32 devices in a mesh: segment: 4 (over y, x), feat: 4 (over z), tok: 2 (over core).
Axes of the slice: x: 2, y: 2, z: 4, core: 2. Of those that a mesh axis runs over, the one named last changes fastest.
Arguments:
- layer_inputs: bfloat16 [4, 448, 2304], P('segment', 'feat', 'tok'), may hold values from -6 to 6
- targets: bfloat16 [4, 448, 2304], P('segment', 'tok', 'feat'), may hold values from -6 to 6
- enc_weight: bfloat16 [4, 2304, 12288], P('segment', 'feat', 'tok'), may hold values from -0.125 to 0.125
- enc_bias: float32 [4, 12288], P('segment', 'tok'), may hold values from -3 to 3
- dec_weight: bfloat16 [4, 4, 2304, 12288], P('segment', None, 'feat', 'tok'), may hold values from -0.0546875 to 0.0546875
Outputs:
- features: bfloat16 [4, 448, 12288], P('segment', 'feat', 'tok')
- residual: float32 [4, 448, 2304], P('segment', 'tok', 'feat')
The draws below stay inside these ranges and needn't reach their ends.
All inputs are finite; a program needn't handle non-finite values.
Results may differ from the reference program's by a relative error of at most 0.01.
Values may be sent and summed in bfloat16 or wider, within the bound.
No kernel may reach another device: no remote copies, remote signals or barrier semaphores. Data moves between devices by JAX's collectives and lax.ppermute only.
A program may use at most 128 MiB of HBM per device.

```python
import jax
import jax.numpy as jnp
from jax import lax

D = 2304
F = 12288
LAYERS = 4
TOKENS = 448


def shard_levels(rng, extent, pieces, least, top_value):
    gain = 1.0
    for dim, parts in pieces:
        steps = jax.random.uniform(jax.random.fold_in(jax.random.fold_in(rng, 6), dim), (parts,), jnp.float32, least / len(pieces), top_value / len(pieces))
        gain = gain * jnp.repeat(jnp.exp(steps), extent[dim] // parts).reshape((-1,) + (1,) * (len(extent) - 1 - dim))
    return gain


def noise(own_key, extent, spread, limit, split=(), kind=jnp.bfloat16):
    values = jax.random.normal(own_key, extent, jnp.float32) * spread
    if len(split) > 0:
        values = shard_levels(own_key, extent, split, -0.22, 0.18) * values
    return jnp.clip(values, min=-limit, max=limit).astype(kind)


def setup_inputs(seed: int = 0) -> dict:
    key_list = jax.random.split(jax.random.key(seed), 6)
    return {
        "layer_inputs": noise(key_list[0], (LAYERS, TOKENS, D), 1.0, 6.0, ((0, 4), (1, 4), (2, 2))),
        "targets": noise(key_list[1], (LAYERS, TOKENS, D), 1.0, 6.0, ((0, 4), (1, 2), (2, 4))),
        "enc_weight": noise(key_list[2], (LAYERS, D, F), D ** -0.5, 0.125, ((0, 4), (1, 4), (2, 2))),
        "enc_bias": noise(key_list[3], (LAYERS, F), 0.5, 3.0, ((0, 4), (1, 2)), jnp.float32),
        "dec_weight": noise(key_list[4], (LAYERS, LAYERS, D, F), F ** -0.5, 0.0546875, ((0, 4), (2, 4), (3, 2))),
    }


def reference(layer_inputs, targets, enc_weight, enc_bias, dec_weight):
    codes = []
    for source in range(LAYERS):
        preact = jnp.dot(layer_inputs[source], enc_weight[source], preferred_element_type=jnp.float32)
        code = jax.nn.relu(preact + enc_bias[source][None, :]).astype(jnp.bfloat16)
        codes.append(code)
    residuals = []
    for target in range(LAYERS):
        rebuilt = jnp.zeros((TOKENS, D), jnp.float32)
        for source in range(target + 1):
            rebuilt = rebuilt + lax.dot_general(codes[source], dec_weight[source, target], (((1,), (1,)), ((), ())), preferred_element_type=jnp.float32)
        residuals.append(targets[target].astype(jnp.float32) - rebuilt)
    return jnp.stack(codes), jnp.stack(residuals)
```

```python
import jax
import jax.numpy as jnp
from jax import lax
from jax.sharding import PartitionSpec as P


def local(layer_inputs, targets, enc_weight, enc_bias, dec_weight):
    segment_index = lax.axis_index("segment")
    rows = lax.all_gather(layer_inputs[0], "tok", axis=1, tiled=True)
    columns = lax.all_to_all(rows, "feat", split_axis=1, concat_axis=0, tiled=True)
    partial = jnp.dot(columns, enc_weight[0], preferred_element_type=jnp.float32)
    preact = lax.psum_scatter(
        partial.astype(jnp.bfloat16), "feat", scatter_dimension=0, tiled=True
    ).astype(jnp.float32)
    features = jax.nn.relu(preact + enc_bias[0][None, :]).astype(jnp.bfloat16)
    all_codes = lax.all_gather(features, "feat", axis=0, tiled=True)
    decoders = dec_weight[0]
    layers = decoders.shape[0]
    target_mask = (jnp.arange(layers) >= segment_index).astype(jnp.float32)
    decoded = jnp.einsum("nf,ldf->nld", all_codes, decoders, preferred_element_type=jnp.float32)
    contrib = lax.psum_scatter(
        (decoded * target_mask[None, :, None]).astype(jnp.bfloat16),
        "tok",
        scatter_dimension=0,
        tiled=True,
    ).astype(jnp.float32)
    routed = lax.all_to_all(
        contrib.astype(jnp.bfloat16), "segment", split_axis=1, concat_axis=1, tiled=True
    ).astype(contrib.dtype)
    own_recon = jnp.sum(routed, axis=1)
    residual = targets[0].astype(jnp.float32) - own_recon
    return (features[None], residual[None])


def solution(mesh):
    in_specs = (
        P("segment", "feat", "tok"),
        P("segment", "tok", "feat"),
        P("segment", "feat", "tok"),
        P("segment", "tok"),
        P("segment", None, "feat", "tok"),
    )
    out_specs = (P("segment", "feat", "tok"), P("segment", "tok", "feat"))
    return jax.shard_map(local, mesh=mesh, in_specs=in_specs, out_specs=out_specs, check_vma=False)
```

```python
import jax
import jax.numpy as jnp
from jax import lax
from jax.sharding import PartitionSpec as P

BF16 = jnp.bfloat16
F32 = jnp.float32
GROUPS = 2
CHUNKS = 4
STREAMS = 2


def local(segments, ring, cores, layer_inputs, targets, enc_weight, enc_bias, dec_weight):
    z = lax.axis_index("feat")
    core = lax.axis_index("tok")
    segment = lax.axis_index("segment")
    rows = layer_inputs.shape[1] // GROUPS
    width = enc_weight.shape[2] // CHUNKS
    depth = enc_weight.shape[1]
    weight = enc_weight[0]
    decoders = dec_weight[0]
    layers = decoders.shape[0]
    per_core = ring // cores

    own_rows = lax.all_gather(layer_inputs[0], "tok", axis=1, tiled=True)

    def exchanged(group):
        block = own_rows[group * rows : (group + 1) * rows]
        parts = []
        for k in range(ring):
            part = lax.dynamic_slice_in_dim(block, ((z + k) % ring) * depth, depth, axis=1)
            if k:
                part = lax.ppermute(part, "feat", [(i, (i + k) % ring) for i in range(ring)])
            parts.append(part)
        return jnp.concatenate(parts, axis=0)

    columns = [exchanged(group) for group in range(GROUPS)]

    def partial_sums(group, chunk):
        part = jnp.dot(
            columns[group], weight[:, chunk * width : (chunk + 1) * width], preferred_element_type=F32
        )
        return [part[k * rows : (k + 1) * rows] for k in range(ring)]

    units = [(group, chunk) for group in range(GROUPS) for chunk in range(CHUNKS)]
    finished = {}
    decoded = {}

    def decode(unit, codes):
        group, chunk = unit
        all_codes = jnp.concatenate(codes, axis=0)
        out = jnp.einsum(
            "nf,ldf->lnd",
            all_codes,
            decoders[:, :, chunk * width : (chunk + 1) * width],
            preferred_element_type=F32,
        )
        decoded[group] = out if group not in decoded else decoded[group] + out

    class Stream:
        def __init__(self, own):
            self.own = own
            self.step = 0
            self.slot = 1
            self.right = {0: None}
            self.left = {0: None}
            self.sums = partial_sums(*own[0])

        def advance(self):
            i, k, n = self.step, self.slot, len(self.own)
            if k == 0:
                send_right = send_left = finished[self.own[i - 1]]
            else:
                send_right, send_left = self.right[k - 1], self.left[k - 1]
                if i < n:
                    add_right = jnp.where(k > z, self.sums[k], 0.0)
                    add_left = jnp.where(k > ring - 1 - z, self.sums[ring - k], 0.0)
                    if send_right is not None:
                        add_right += send_right.astype(F32)
                        add_left += send_left.astype(F32)
                    send_right, send_left = add_right.astype(BF16), add_left.astype(BF16)
            places = range(ring - 1)
            if i == 0:
                places = [p for p in places if p < k]
            if i == n:
                places = [p for p in places if p >= k]
            self.right[k] = lax.ppermute(send_right, "feat", [(p, p + 1) for p in places])
            self.left[k] = lax.ppermute(send_left, "feat", [(ring - 1 - p, ring - 2 - p) for p in places])
            if i and k == ring - 2:
                unit = self.own[i - 1]
                codes = [finished[unit]]
                for m in range(1, ring):
                    codes.append(jnp.where(m <= z, self.right[m - 1], self.left[ring - m - 1]))
                decode(unit, codes)
            self.slot += 1
            if i < n and k == ring - 1:
                chunk = self.own[i][1]
                bias = enc_bias[0, chunk * width : (chunk + 1) * width][None, :]
                total = self.sums[0] + self.right[k].astype(F32) + self.left[k].astype(F32)
                finished[self.own[i]] = jax.nn.relu(total + bias).astype(BF16)
                self.slot, self.step = 0, i + 1
                if i + 1 < n:
                    self.sums = partial_sums(*self.own[i + 1])
                self.right, self.left = {}, {}
                return True
            return not (i == n and k == ring - 2)

    def residual_rows(group):
        blocks = decoded[group].reshape(layers, ring, rows, depth)

        def share(index):
            first = index * per_core
            return jnp.stack(
                [
                    lax.dynamic_index_in_dim(blocks, (z - first - b) % ring, axis=1, keepdims=False)
                    for b in range(per_core)
                ],
                axis=1,
            )

        total = share(core)
        for k in range(1, cores):
            sent = share((core + k) % cores).astype(BF16)
            total += lax.ppermute(sent, "tok", [(i, (i + k) % cores) for i in range(cores)]).astype(F32)
        own = lax.dynamic_index_in_dim(total, segment, axis=0, keepdims=False)
        for k in range(1, segments):
            place = jnp.minimum(segment + k, layers - 1)
            sent = lax.dynamic_index_in_dim(total, place, axis=0, keepdims=False).astype(BF16)
            own += lax.ppermute(sent, "segment", [(i, i + k) for i in range(segments - k)]).astype(F32)
        return own

    streams = [Stream(units[i::STREAMS]) for i in range(STREAMS)]
    going = [True] * STREAMS
    results = {}
    while any(going):
        for i, stream in enumerate(streams):
            if going[i]:
                going[i] = stream.advance()
    own = jnp.stack([residual_rows(group) for group in range(GROUPS)], axis=1)
    residual = targets[0].astype(F32) - own.reshape(targets.shape[1:])
    features = jnp.concatenate(
        [
            jnp.concatenate([finished[group, chunk] for chunk in range(CHUNKS)], axis=1)
            for group in range(GROUPS)
        ],
        axis=0,
    )
    return (features[None], residual[None])


def solution(mesh):
    in_specs = (
        P("segment", "feat", "tok"),
        P("segment", "tok", "feat"),
        P("segment", "feat", "tok"),
        P("segment", "tok"),
        P("segment", None, "feat", "tok"),
    )
    out_specs = (P("segment", "feat", "tok"), P("segment", "tok", "feat"))
    sizes = (mesh.shape["segment"], mesh.shape["feat"], mesh.shape["tok"])
    return jax.shard_map(
        lambda *args: local(*sizes, *args), mesh=mesh, in_specs=in_specs, out_specs=out_specs, check_vma=False
    )
```

```python
import jax
import jax.numpy as jnp
from jax import lax
from jax.sharding import PartitionSpec as P

BF16 = jnp.bfloat16
F32 = jnp.float32
GROUPS = 2
CHUNKS = 2


def local(segments, ring, cores, layer_inputs, targets, enc_weight, enc_bias, dec_weight):
    z = lax.axis_index("feat")
    core = lax.axis_index("tok")
    segment = lax.axis_index("segment")
    rows = layer_inputs.shape[1] // GROUPS
    width = enc_weight.shape[2] // CHUNKS
    depth = enc_weight.shape[1]
    weight = enc_weight[0]
    decoders = dec_weight[0]
    layers = decoders.shape[0]
    per_core = ring // cores

    own_rows = lax.all_gather(layer_inputs[0], "tok", axis=1, tiled=True)

    def exchanged(group):
        block = own_rows[group * rows : (group + 1) * rows]
        parts = []
        for k in range(ring):
            part = lax.dynamic_slice_in_dim(block, ((z + k) % ring) * depth, depth, axis=1)
            if k:
                part = lax.ppermute(part, "feat", [(i, (i + k) % ring) for i in range(ring)])
            parts.append(part)
        parts = jnp.stack(parts)
        return jnp.concatenate(
            [lax.dynamic_slice_in_dim(parts, (z - i) % ring, 1, axis=0)[0] for i in range(ring)], axis=0
        )

    columns = [exchanged(group) for group in range(GROUPS)]
    units = [(group, chunk) for group in range(GROUPS) for chunk in range(CHUNKS)]
    finished = {}
    decoded = {}
    for group, chunk in units:
        span = slice(chunk * width, (chunk + 1) * width)
        part = jnp.dot(columns[group], weight[:, span], preferred_element_type=F32)
        preact = lax.psum_scatter(part.astype(BF16), "feat", scatter_dimension=0, tiled=True).astype(F32)
        codes = jax.nn.relu(preact + enc_bias[0, span][None, :]).astype(BF16)
        finished[group, chunk] = codes
        all_codes = lax.all_gather(codes, "feat", axis=0, tiled=True)
        out = jnp.einsum("nf,ldf->lnd", all_codes, decoders[:, :, span], preferred_element_type=F32)
        decoded[group] = out if group not in decoded else decoded[group] + out

    def residual_rows(group):
        blocks = decoded[group].reshape(layers, ring, rows, depth)

        def share(index):
            return lax.dynamic_slice_in_dim(blocks, index * per_core, per_core, axis=1)

        total = share(core)
        for k in range(1, cores):
            sent = share((core + k) % cores).astype(BF16)
            total += lax.ppermute(sent, "tok", [(i, (i + k) % cores) for i in range(cores)]).astype(F32)
        own = lax.dynamic_index_in_dim(total, segment, axis=0, keepdims=False)
        for k in range(1, segments):
            place = jnp.minimum(segment + k, layers - 1)
            sent = lax.dynamic_index_in_dim(total, place, axis=0, keepdims=False).astype(BF16)
            own += lax.ppermute(sent, "segment", [(i, i + k) for i in range(segments - k)]).astype(F32)
        return own

    own = jnp.stack([residual_rows(group) for group in range(GROUPS)], axis=1)
    residual = targets[0].astype(F32) - own.reshape(targets.shape[1:])
    features = jnp.concatenate(
        [
            jnp.concatenate([finished[group, chunk] for chunk in range(CHUNKS)], axis=1)
            for group in range(GROUPS)
        ],
        axis=0,
    )
    return (features[None], residual[None])


def solution(mesh):
    in_specs = (
        P("segment", "feat", "tok"),
        P("segment", "tok", "feat"),
        P("segment", "feat", "tok"),
        P("segment", "tok"),
        P("segment", None, "feat", "tok"),
    )
    out_specs = (P("segment", "feat", "tok"), P("segment", "tok", "feat"))
    sizes = (mesh.shape["segment"], mesh.shape["feat"], mesh.shape["tok"])
    return jax.shard_map(
        lambda *args: local(*sizes, *args), mesh=mesh, in_specs=in_specs, out_specs=out_specs, check_vma=False
    )
```

```python
import jax
import jax.numpy as jnp
from jax import lax
from jax.sharding import PartitionSpec as P

BF16 = jnp.bfloat16
F32 = jnp.float32
GROUPS = 2
CHUNKS = 2
STREAMS = 2


def local(segments, ring, cores, layer_inputs, targets, enc_weight, enc_bias, dec_weight):
    z = lax.axis_index("feat")
    core = lax.axis_index("tok")
    segment = lax.axis_index("segment")
    odd = z % 2 == 1
    rows = layer_inputs.shape[1] // GROUPS
    width = enc_weight.shape[2] // CHUNKS
    depth = enc_weight.shape[1]
    weight = enc_weight[0]
    decoders = dec_weight[0]
    layers = decoders.shape[0]
    per_core = ring // cores

    own_rows = lax.all_gather(layer_inputs[0], "tok", axis=1, tiled=True)

    def exchanged(group):
        block = own_rows[group * rows : (group + 1) * rows]
        parts = []
        for k in range(ring):
            part = lax.dynamic_slice_in_dim(block, ((z + k) % ring) * depth, depth, axis=1)
            if k:
                part = lax.ppermute(part, "feat", [(i, (i + k) % ring) for i in range(ring)])
            parts.append(part)
        return jnp.concatenate(parts, axis=0)

    columns = [exchanged(group) for group in range(GROUPS)]

    def partial_sums(group, chunk):
        part = jnp.dot(
            columns[group], weight[:, chunk * width : (chunk + 1) * width], preferred_element_type=F32
        )
        return [part[k * rows : (k + 1) * rows] for k in range(ring)]

    units = [(group, chunk) for group in range(GROUPS) for chunk in range(CHUNKS)]
    finished = {}
    decoded = {}

    def decode(unit, codes):
        group, chunk = unit
        all_codes = jnp.concatenate(codes, axis=0)
        out = jnp.einsum(
            "nf,ldf->lnd",
            all_codes,
            decoders[:, :, chunk * width : (chunk + 1) * width],
            preferred_element_type=F32,
        )
        decoded[group] = out if group not in decoded else decoded[group] + out

    class Stream:
        def __init__(self, own):
            self.own = own
            self.step = 0
            self.slot = 1
            self.got = [{}, {}]
            self.sums = partial_sums(*own[0])

        def swap(self, value, side):
            i, k, n = self.step, self.slot, len(self.own)
            pairs = []
            for p in range(side, ring - 1, 2):
                q = ring - 2 - p
                if not (i == 0 and p >= k or i == n and p < k):
                    pairs.append((p, p + 1))
                if not (i == 0 and q >= k or i == n and q < k):
                    pairs.append((p + 1, p))
            return lax.ppermute(value, "feat", pairs) if pairs else None

        def advance(self):
            i, k, n = self.step, self.slot, len(self.own)
            sent = []
            for side in range(2):
                if k == 0:
                    sent.append(finished[self.own[i - 1]])
                    continue
                value = self.got[1 - side].get(k - 1)
                if i < n:
                    rightward = odd == (side == 1)
                    own = jnp.where(
                        rightward,
                        jnp.where(k > z, self.sums[k], 0.0),
                        jnp.where(k > ring - 1 - z, self.sums[ring - k], 0.0),
                    )
                    value = (own if value is None else own + value.astype(F32)).astype(BF16)
                sent.append(value)
            for side in range(2):
                got = self.swap(sent[side], side) if sent[side] is not None else None
                if got is not None:
                    self.got[side][k] = got
            if i and k == ring - 2:
                unit = self.own[i - 1]
                codes = [finished[unit]]
                zero = jnp.zeros_like(codes[0])
                for m in range(1, ring):
                    a, b = m - 1, ring - m - 1
                    left = jnp.where(odd, self.got[0].get(a, zero), self.got[1].get(a, zero))
                    right = jnp.where(odd, self.got[1].get(b, zero), self.got[0].get(b, zero))
                    codes.append(jnp.where(m <= z, left, right))
                decode(unit, codes)
            self.slot += 1
            if i < n and k == ring - 1:
                chunk = self.own[i][1]
                bias = enc_bias[0, chunk * width : (chunk + 1) * width][None, :]
                total = self.sums[0] + self.got[0][k].astype(F32) + self.got[1][k].astype(F32)
                finished[self.own[i]] = jax.nn.relu(total + bias).astype(BF16)
                self.slot, self.step = 0, i + 1
                if i + 1 < n:
                    self.sums = partial_sums(*self.own[i + 1])
                self.got = [{}, {}]
                return True
            return not (i == n and k == ring - 2)

    def residual_rows(group):
        blocks = decoded[group].reshape(layers, ring, rows, depth)

        def share(index):
            first = index * per_core
            return jnp.stack(
                [
                    lax.dynamic_index_in_dim(blocks, (z - first - b) % ring, axis=1, keepdims=False)
                    for b in range(per_core)
                ],
                axis=1,
            )

        total = share(core)
        for k in range(1, cores):
            sent = share((core + k) % cores).astype(BF16)
            total += lax.ppermute(sent, "tok", [(i, (i + k) % cores) for i in range(cores)]).astype(F32)
        own = lax.dynamic_index_in_dim(total, segment, axis=0, keepdims=False)
        for k in range(1, segments):
            place = jnp.minimum(segment + k, layers - 1)
            sent = lax.dynamic_index_in_dim(total, place, axis=0, keepdims=False).astype(BF16)
            own += lax.ppermute(sent, "segment", [(i, i + k) for i in range(segments - k)]).astype(F32)
        return own

    streams = [Stream(units[i::STREAMS]) for i in range(STREAMS)]
    going = [True] * STREAMS
    while any(going):
        for i, stream in enumerate(streams):
            if going[i]:
                going[i] = stream.advance()
    own = jnp.stack([residual_rows(group) for group in range(GROUPS)], axis=1)
    residual = targets[0].astype(F32) - own.reshape(targets.shape[1:])
    features = jnp.concatenate(
        [
            jnp.concatenate([finished[group, chunk] for chunk in range(CHUNKS)], axis=1)
            for group in range(GROUPS)
        ],
        axis=0,
    )
    return (features[None], residual[None])


def solution(mesh):
    in_specs = (
        P("segment", "feat", "tok"),
        P("segment", "tok", "feat"),
        P("segment", "feat", "tok"),
        P("segment", "tok"),
        P("segment", None, "feat", "tok"),
    )
    out_specs = (P("segment", "feat", "tok"), P("segment", "tok", "feat"))
    sizes = (mesh.shape["segment"], mesh.shape["feat"], mesh.shape["tok"])
    return jax.shard_map(
        lambda *args: local(*sizes, *args), mesh=mesh, in_specs=in_specs, out_specs=out_specs, check_vma=False
    )
```

```python
import jax
import jax.numpy as jnp
from jax import lax
from jax.sharding import PartitionSpec as P

BF16 = jnp.bfloat16
F32 = jnp.float32
GROUPS = 2
CHUNKS = 2
STREAMS = 2


def local(segments, ring, cores, layer_inputs, targets, enc_weight, enc_bias, dec_weight):
    z = lax.axis_index("feat")
    core = lax.axis_index("tok")
    segment = lax.axis_index("segment")
    odd = z % 2 == 1
    rows = layer_inputs.shape[1] // GROUPS
    width = enc_weight.shape[2] // CHUNKS
    depth = enc_weight.shape[1]
    weight = enc_weight[0]
    decoders = dec_weight[0]
    layers = decoders.shape[0]
    per_core = ring // cores

    own_rows = lax.all_gather(layer_inputs[0], "tok", axis=1, tiled=True)

    def exchanged(group):
        block = own_rows[group * rows : (group + 1) * rows]
        parts = []
        for k in range(ring):
            part = lax.dynamic_slice_in_dim(block, ((z + k) % ring) * depth, depth, axis=1)
            if k:
                part = lax.ppermute(part, "feat", [(i, (i + k) % ring) for i in range(ring)])
            parts.append(part)
        return jnp.concatenate(parts, axis=0)

    columns = [exchanged(group) for group in range(GROUPS)]

    def partial_sums(group, chunk):
        part = jnp.dot(
            columns[group], weight[:, chunk * width : (chunk + 1) * width], preferred_element_type=F32
        )
        return [part[k * rows : (k + 1) * rows] for k in range(ring)]

    units = [(group, chunk) for group in range(GROUPS) for chunk in range(CHUNKS)]
    finished = {}
    decoded = {}
    waiting = []
    ordered = [None]
    left = {group: CHUNKS * layers for group in range(GROUPS)}
    totals = {}
    residuals = {}

    def after(values, others):
        others = [x for x in jax.tree.leaves(others) if x is not None]
        return lax.optimization_barrier((values, others))[0] if others else values

    def background(sent):
        if waiting:
            ordered[0] = waiting.pop(0)(sent)

    def decode(unit, codes):
        group, chunk = unit

        def piece(layer):
            def run(sent):
                all_codes = after(codes_of[0], sent)
                out = lax.dot_general(
                    all_codes,
                    decoders[layer, :, chunk * width : (chunk + 1) * width],
                    (((1,), (1,)), ((), ())),
                    preferred_element_type=F32,
                )
                key = group, layer
                decoded[key] = out if key not in decoded else decoded[key] + out
                left[group] -= 1
                if not left[group]:
                    waiting.extend([lambda sent: share_cores(group, sent), lambda sent: share_segments(group, sent)])
                return decoded[key]

            return run

        codes_of = [jnp.concatenate(codes, axis=0)]
        waiting.extend(piece(layer) for layer in reversed(range(layers)))

    class Stream:
        def __init__(self, own):
            self.own = own
            self.step = 0
            self.slot = 1
            self.got = [{}, {}]
            self.sums = partial_sums(*own[0])

        def swap(self, value, side):
            i, k, n = self.step, self.slot, len(self.own)
            pairs = []
            for p in range(side, ring - 1, 2):
                q = ring - 2 - p
                if not (i == 0 and p >= k or i == n and p < k):
                    pairs.append((p, p + 1))
                if not (i == 0 and q >= k or i == n and q < k):
                    pairs.append((p + 1, p))
            return lax.ppermute(value, "feat", pairs) if pairs else None

        def advance(self):
            i, k, n = self.step, self.slot, len(self.own)
            sent = []
            for side in range(2):
                if k == 0:
                    sent.append(finished[self.own[i - 1]])
                    continue
                value = self.got[1 - side].get(k - 1)
                if value is not None:
                    value = after(value, ordered)
                if i < n:
                    rightward = odd == (side == 1)
                    own = jnp.where(
                        rightward,
                        jnp.where(k > z, self.sums[k], 0.0),
                        jnp.where(k > ring - 1 - z, self.sums[ring - k], 0.0),
                    )
                    value = (own if value is None else own + value.astype(F32)).astype(BF16)
                sent.append(value)
            for side in range(2):
                got = self.swap(sent[side], side) if sent[side] is not None else None
                if got is not None:
                    self.got[side][k] = got
            background(sent)
            if i and k == ring - 2:
                unit = self.own[i - 1]
                codes = [finished[unit]]
                zero = jnp.zeros_like(codes[0])
                for m in range(1, ring):
                    a, b = m - 1, ring - m - 1
                    left = jnp.where(odd, self.got[0].get(a, zero), self.got[1].get(a, zero))
                    right = jnp.where(odd, self.got[1].get(b, zero), self.got[0].get(b, zero))
                    codes.append(jnp.where(m <= z, left, right))
                decode(unit, codes)
            self.slot += 1
            if i < n and k == ring - 1:
                chunk = self.own[i][1]
                bias = enc_bias[0, chunk * width : (chunk + 1) * width][None, :]
                total = self.sums[0] + self.got[0][k].astype(F32) + self.got[1][k].astype(F32)
                finished[self.own[i]] = jax.nn.relu(total + bias).astype(BF16)
                self.slot, self.step = 0, i + 1
                if i + 1 < n:
                    self.sums = partial_sums(*self.own[i + 1])
                self.got = [{}, {}]
                return True
            return not (i == n and k == ring - 2)

    def share_cores(group, sent):
        blocks = after([decoded[group, layer] for layer in range(layers)], sent)
        blocks = jnp.stack(blocks).reshape(layers, ring, rows, depth)

        def share(index):
            first = index * per_core
            return jnp.stack(
                [
                    lax.dynamic_index_in_dim(blocks, (z - first - b) % ring, axis=1, keepdims=False)
                    for b in range(per_core)
                ],
                axis=1,
            )

        total = share(core)
        given = []
        for k in range(1, cores):
            given.append(share((core + k) % cores).astype(BF16))
            got = lax.ppermute(given[-1], "tok", [(i, (i + k) % cores) for i in range(cores)])
            total += got.astype(F32)
        totals[group] = total
        return given

    def share_segments(group, sent):
        total = after(totals[group], sent)
        own = lax.dynamic_index_in_dim(total, segment, axis=0, keepdims=False)
        given = []
        for k in range(1, segments):
            place = jnp.minimum(segment + k, layers - 1)
            given.append(lax.dynamic_index_in_dim(total, place, axis=0, keepdims=False).astype(BF16))
            got = lax.ppermute(given[-1], "segment", [(i, i + k) for i in range(segments - k)])
            own += got.astype(F32)
        residuals[group] = own
        return given

    streams = [Stream(units[i::STREAMS]) for i in range(STREAMS)]
    going = [True] * STREAMS
    while any(going):
        for i, stream in enumerate(streams):
            if going[i]:
                going[i] = stream.advance()
    while waiting:
        background(None)
    own = jnp.stack([residuals[group] for group in range(GROUPS)], axis=1)
    residual = targets[0].astype(F32) - own.reshape(targets.shape[1:])
    features = jnp.concatenate(
        [
            jnp.concatenate([finished[group, chunk] for chunk in range(CHUNKS)], axis=1)
            for group in range(GROUPS)
        ],
        axis=0,
    )
    return (features[None], residual[None])


def solution(mesh):
    in_specs = (
        P("segment", "feat", "tok"),
        P("segment", "tok", "feat"),
        P("segment", "feat", "tok"),
        P("segment", "tok"),
        P("segment", None, "feat", "tok"),
    )
    out_specs = (P("segment", "feat", "tok"), P("segment", "tok", "feat"))
    sizes = (mesh.shape["segment"], mesh.shape["feat"], mesh.shape["tok"])
    return jax.shard_map(
        lambda *args: local(*sizes, *args), mesh=mesh, in_specs=in_specs, out_specs=out_specs, check_vma=False
    )
```

```python
import jax
import jax.numpy as jnp
from jax import lax
from jax.sharding import PartitionSpec as P

BF16 = jnp.bfloat16
F32 = jnp.float32
GROUPS = 2
CHUNKS = 4
PIECES = 2
STREAMS = 2


def local(segments, ring, cores, layer_inputs, targets, enc_weight, enc_bias, dec_weight):
    z = lax.axis_index("feat")
    core = lax.axis_index("tok")
    segment = lax.axis_index("segment")
    odd = z % 2 == 1
    rows = layer_inputs.shape[1] // GROUPS
    width = enc_weight.shape[2] // CHUNKS
    depth = enc_weight.shape[1]
    weight = enc_weight[0]
    decoders = dec_weight[0]
    layers = decoders.shape[0]
    per_core = ring // cores

    own_rows = lax.all_gather(layer_inputs[0], "tok", axis=1, tiled=True)

    def exchanged(group):
        block = own_rows[group * rows : (group + 1) * rows]
        parts = []
        for k in range(ring):
            part = lax.dynamic_slice_in_dim(block, ((z + k) % ring) * depth, depth, axis=1)
            if k:
                part = lax.ppermute(part, "feat", [(i, (i + k) % ring) for i in range(ring)])
            parts.append(part)
        return jnp.concatenate(parts, axis=0)

    columns = [exchanged(group) for group in range(GROUPS)]

    def partial_sums(group, chunk):
        part = jnp.dot(
            columns[group], weight[:, chunk * width : (chunk + 1) * width], preferred_element_type=F32
        )
        return [part[k * rows : (k + 1) * rows] for k in range(ring)]

    units = [(group, chunk) for group in range(GROUPS) for chunk in range(CHUNKS)]
    finished = {}
    decoded = {}
    waiting = []
    ordered = [None]
    left = {group: CHUNKS * layers for group in range(GROUPS)}
    totals = {}
    residuals = {}

    def after(values, others):
        others = [x for x in jax.tree.leaves(others) if x is not None]
        return lax.optimization_barrier((values, others))[0] if others else values

    def background(sent):
        for _ in range(min(PIECES, len(waiting))):
            ordered[0] = sent = waiting.pop(0)(sent)

    def decode(unit, codes):
        group, chunk = unit

        def piece(layer):
            def run(sent):
                all_codes = after(codes_of[0], sent)
                out = lax.dot_general(
                    all_codes,
                    decoders[layer, :, chunk * width : (chunk + 1) * width],
                    (((1,), (1,)), ((), ())),
                    preferred_element_type=F32,
                )
                key = group, layer
                decoded[key] = out if key not in decoded else decoded[key] + out
                left[group] -= 1
                if not left[group]:
                    waiting.extend([lambda sent: share_cores(group, sent), lambda sent: share_segments(group, sent)])
                return decoded[key]

            return run

        codes_of = [jnp.concatenate(codes, axis=0)]
        waiting.extend(piece(layer) for layer in reversed(range(layers)))

    class Stream:
        def __init__(self, own):
            self.own = own
            self.step = 0
            self.slot = 1
            self.got = [{}, {}]
            self.sums = partial_sums(*own[0])

        def swap(self, value, side):
            i, k, n = self.step, self.slot, len(self.own)
            pairs = []
            for p in range(side, ring - 1, 2):
                q = ring - 2 - p
                if not (i == 0 and p >= k or i == n and p < k):
                    pairs.append((p, p + 1))
                if not (i == 0 and q >= k or i == n and q < k):
                    pairs.append((p + 1, p))
            return lax.ppermute(value, "feat", pairs) if pairs else None

        def advance(self):
            i, k, n = self.step, self.slot, len(self.own)
            sent = []
            for side in range(2):
                if k == 0:
                    sent.append(finished[self.own[i - 1]])
                    continue
                value = self.got[1 - side].get(k - 1)
                if value is not None:
                    value = after(value, ordered)
                if i < n:
                    rightward = odd == (side == 1)
                    own = jnp.where(
                        rightward,
                        jnp.where(k > z, self.sums[k], 0.0),
                        jnp.where(k > ring - 1 - z, self.sums[ring - k], 0.0),
                    )
                    value = (own if value is None else own + value.astype(F32)).astype(BF16)
                sent.append(value)
            for side in range(2):
                got = self.swap(sent[side], side) if sent[side] is not None else None
                if got is not None:
                    self.got[side][k] = got
            background(sent)
            if i and k == ring - 2:
                unit = self.own[i - 1]
                codes = [finished[unit]]
                zero = jnp.zeros_like(codes[0])
                for m in range(1, ring):
                    a, b = m - 1, ring - m - 1
                    left = jnp.where(odd, self.got[0].get(a, zero), self.got[1].get(a, zero))
                    right = jnp.where(odd, self.got[1].get(b, zero), self.got[0].get(b, zero))
                    codes.append(jnp.where(m <= z, left, right))
                decode(unit, codes)
            self.slot += 1
            if i < n and k == ring - 1:
                chunk = self.own[i][1]
                bias = enc_bias[0, chunk * width : (chunk + 1) * width][None, :]
                total = self.sums[0] + self.got[0][k].astype(F32) + self.got[1][k].astype(F32)
                finished[self.own[i]] = jax.nn.relu(total + bias).astype(BF16)
                self.slot, self.step = 0, i + 1
                if i + 1 < n:
                    self.sums = partial_sums(*self.own[i + 1])
                self.got = [{}, {}]
                return True
            return not (i == n and k == ring - 2)

    def share_cores(group, sent):
        blocks = after([decoded[group, layer] for layer in range(layers)], sent)
        blocks = jnp.stack(blocks).reshape(layers, ring, rows, depth)

        def share(index):
            first = index * per_core
            return jnp.stack(
                [
                    lax.dynamic_index_in_dim(blocks, (z - first - b) % ring, axis=1, keepdims=False)
                    for b in range(per_core)
                ],
                axis=1,
            )

        total = share(core)
        given = []
        for k in range(1, cores):
            given.append(share((core + k) % cores).astype(BF16))
            got = lax.ppermute(given[-1], "tok", [(i, (i + k) % cores) for i in range(cores)])
            total += got.astype(F32)
        totals[group] = total
        return given

    def share_segments(group, sent):
        total = after(totals[group], sent)
        own = lax.dynamic_index_in_dim(total, segment, axis=0, keepdims=False)
        given = []
        for k in range(1, segments):
            place = jnp.minimum(segment + k, layers - 1)
            given.append(lax.dynamic_index_in_dim(total, place, axis=0, keepdims=False).astype(BF16))
            got = lax.ppermute(given[-1], "segment", [(i, i + k) for i in range(segments - k)])
            own += got.astype(F32)
        residuals[group] = own
        return given

    streams = [Stream(units[i::STREAMS]) for i in range(STREAMS)]
    going = [True] * STREAMS
    while any(going):
        for i, stream in enumerate(streams):
            if going[i]:
                going[i] = stream.advance()
    while waiting:
        background(None)
    own = jnp.stack([residuals[group] for group in range(GROUPS)], axis=1)
    residual = targets[0].astype(F32) - own.reshape(targets.shape[1:])
    features = jnp.concatenate(
        [
            jnp.concatenate([finished[group, chunk] for chunk in range(CHUNKS)], axis=1)
            for group in range(GROUPS)
        ],
        axis=0,
    )
    return (features[None], residual[None])


def solution(mesh):
    in_specs = (
        P("segment", "feat", "tok"),
        P("segment", "tok", "feat"),
        P("segment", "feat", "tok"),
        P("segment", "tok"),
        P("segment", None, "feat", "tok"),
    )
    out_specs = (P("segment", "feat", "tok"), P("segment", "tok", "feat"))
    sizes = (mesh.shape["segment"], mesh.shape["feat"], mesh.shape["tok"])
    return jax.shard_map(
        lambda *args: local(*sizes, *args), mesh=mesh, in_specs=in_specs, out_specs=out_specs, check_vma=False
    )
```

```python
import jax
import jax.numpy as jnp
from jax import lax
from jax.sharding import PartitionSpec as P

BF16 = jnp.bfloat16
F32 = jnp.float32
GROUPS = 2
CHUNKS = 2
PIECES = 2
STREAMS = 2


def local(segments, ring, cores, layer_inputs, targets, enc_weight, enc_bias, dec_weight):
    z = lax.axis_index("feat")
    core = lax.axis_index("tok")
    segment = lax.axis_index("segment")
    odd = z % 2 == 1
    rows = layer_inputs.shape[1] // GROUPS
    width = enc_weight.shape[2] // CHUNKS
    depth = enc_weight.shape[1]
    weight = enc_weight[0]
    decoders = dec_weight[0]
    layers = decoders.shape[0]
    per_core = ring // cores

    units = [(group, chunk) for group in range(GROUPS) for chunk in range(CHUNKS)]
    finished = {}
    decoded = {}
    waiting = []
    ordered = [None]
    left = {group: CHUNKS * layers for group in range(GROUPS)}
    totals = {}
    residuals = {}

    def after(values, others):
        others = [x for x in jax.tree.leaves(others) if x is not None]
        return lax.optimization_barrier((values, others))[0] if others else values

    def background(sent):
        for _ in range(min(PIECES, len(waiting))):
            ordered[0] = sent = waiting.pop(0)(sent)

    own_rows = lax.all_gather(layer_inputs[0], "tok", axis=1, tiled=True)
    swaps = ring & (ring - 1) == 0

    def exchanged(group, others):
        block = after(own_rows[group * rows : (group + 1) * rows], others)
        parts, given = [], []
        for k in range(ring):
            to = z ^ k if swaps else (z + k) % ring
            part = lax.dynamic_slice_in_dim(block, to * depth, depth, axis=1)
            given.append(part)
            if k:
                pairs = [(i, i ^ k if swaps else (i + k) % ring) for i in range(ring)]
                part = lax.ppermute(part, "feat", pairs)
            parts.append(part)
        if swaps:
            both = jnp.stack(parts)
            parts = [
                lax.dynamic_index_in_dim(both, z ^ ((z - k) % ring), axis=0, keepdims=False) for k in range(ring)
            ]
        columns[group] = jnp.concatenate(parts, axis=0)
        return given

    columns = {}
    exchanged(0, None)
    waiting.extend([lambda sent, group=group: exchanged(group, sent) for group in range(1, GROUPS)])

    def partial_sums(group, chunk):
        part = jnp.dot(
            after(columns[group], ordered), weight[:, chunk * width : (chunk + 1) * width], preferred_element_type=F32
        )
        return [part[k * rows : (k + 1) * rows] for k in range(ring)]

    def decode(unit, codes):
        group, chunk = unit

        def piece(layer):
            def run(sent):
                all_codes = after(codes_of[0], sent)
                out = lax.dot_general(
                    all_codes,
                    decoders[layer, :, chunk * width : (chunk + 1) * width],
                    (((1,), (1,)), ((), ())),
                    preferred_element_type=F32,
                )
                key = group, layer
                decoded[key] = out if key not in decoded else decoded[key] + out
                left[group] -= 1
                if not left[group]:
                    waiting.extend([lambda sent: share_cores(group, sent), lambda sent: share_segments(group, sent)])
                return decoded[key]

            return run

        codes_of = [jnp.concatenate(codes, axis=0)]
        waiting.extend(piece(layer) for layer in reversed(range(layers)))

    class Stream:
        def __init__(self, own):
            self.own = own
            self.step = 0
            self.slot = 1
            self.got = [{}, {}]
            self.sums = None

        def swap(self, value, side):
            i, k, n = self.step, self.slot, len(self.own)
            pairs = []
            for p in range(side, ring - 1, 2):
                q = ring - 2 - p
                if not (i == 0 and p >= k or i == n and p < k):
                    pairs.append((p, p + 1))
                if not (i == 0 and q >= k or i == n and q < k):
                    pairs.append((p + 1, p))
            return lax.ppermute(value, "feat", pairs) if pairs else None

        def advance(self):
            i, k, n = self.step, self.slot, len(self.own)
            if self.sums is None:
                self.sums = partial_sums(*self.own[0])
            sent = []
            for side in range(2):
                if k == 0:
                    sent.append(finished[self.own[i - 1]])
                    continue
                value = self.got[1 - side].get(k - 1)
                if value is not None:
                    value = after(value, [ordered, sent])
                if i < n:
                    rightward = odd == (side == 1)
                    own = jnp.where(
                        rightward,
                        jnp.where(k > z, self.sums[k], 0.0),
                        jnp.where(k > ring - 1 - z, self.sums[ring - k], 0.0),
                    )
                    value = (own if value is None else own + value.astype(F32)).astype(BF16)
                sent.append(value)
            for side in range(2):
                got = self.swap(sent[side], side) if sent[side] is not None else None
                if got is not None:
                    self.got[side][k] = got
            if i == 0 and k == 1:
                ordered[0] = sent
            else:
                background(sent)
            if i and k == ring - 2:
                unit = self.own[i - 1]
                codes = [finished[unit]]
                zero = jnp.zeros_like(codes[0])
                for m in range(1, ring):
                    a, b = m - 1, ring - m - 1
                    left = jnp.where(odd, self.got[0].get(a, zero), self.got[1].get(a, zero))
                    right = jnp.where(odd, self.got[1].get(b, zero), self.got[0].get(b, zero))
                    codes.append(jnp.where(m <= z, left, right))
                decode(unit, codes)
            self.slot += 1
            if i < n and k == ring - 1:
                chunk = self.own[i][1]
                bias = enc_bias[0, chunk * width : (chunk + 1) * width][None, :]
                total = self.sums[0] + self.got[0][k].astype(F32) + self.got[1][k].astype(F32)
                finished[self.own[i]] = jax.nn.relu(total + bias).astype(BF16)
                self.slot, self.step = 0, i + 1
                if i + 1 < n:
                    self.sums = partial_sums(*self.own[i + 1])
                self.got = [{}, {}]
                return True
            return not (i == n and k == ring - 2)

    def share_cores(group, sent):
        blocks = after([decoded[group, layer] for layer in range(layers)], sent)
        blocks = jnp.stack(blocks).reshape(layers, ring, rows, depth)

        def share(index):
            first = index * per_core
            return jnp.stack(
                [
                    lax.dynamic_index_in_dim(blocks, (z - first - b) % ring, axis=1, keepdims=False)
                    for b in range(per_core)
                ],
                axis=1,
            )

        total = share(core)
        given = []
        for k in range(1, cores):
            given.append(share((core + k) % cores).astype(BF16))
            got = lax.ppermute(given[-1], "tok", [(i, (i + k) % cores) for i in range(cores)])
            total += got.astype(F32)
        totals[group] = total
        return given

    def share_segments(group, sent):
        total = after(totals[group], sent)
        own = lax.dynamic_index_in_dim(total, segment, axis=0, keepdims=False)
        given = []
        paired = segments & (segments - 1) == 0
        for k in range(1, segments):
            place = segment ^ k if paired else jnp.minimum(segment + k, layers - 1)
            given.append(lax.dynamic_index_in_dim(total, place, axis=0, keepdims=False).astype(BF16))
            pairs = [(i, i ^ k if paired else i + k) for i in range(segments)]
            got = lax.ppermute(given[-1], "segment", [(i, j) for i, j in pairs if i < j < segments])
            own += got.astype(F32)
        residuals[group] = own
        return given

    streams = [Stream(units[i::STREAMS]) for i in range(STREAMS)]
    going = [True] * STREAMS
    while any(going):
        for i, stream in enumerate(streams):
            if going[i]:
                going[i] = stream.advance()
    while waiting:
        background(None)
    own = jnp.stack([residuals[group] for group in range(GROUPS)], axis=1)
    residual = targets[0].astype(F32) - own.reshape(targets.shape[1:])
    features = jnp.concatenate(
        [
            jnp.concatenate([finished[group, chunk] for chunk in range(CHUNKS)], axis=1)
            for group in range(GROUPS)
        ],
        axis=0,
    )
    return (features[None], residual[None])


def solution(mesh):
    in_specs = (
        P("segment", "feat", "tok"),
        P("segment", "tok", "feat"),
        P("segment", "feat", "tok"),
        P("segment", "tok"),
        P("segment", None, "feat", "tok"),
    )
    out_specs = (P("segment", "feat", "tok"), P("segment", "tok", "feat"))
    sizes = (mesh.shape["segment"], mesh.shape["feat"], mesh.shape["tok"])
    return jax.shard_map(
        lambda *args: local(*sizes, *args), mesh=mesh, in_specs=in_specs, out_specs=out_specs, check_vma=False
    )
```

```python
import jax
import jax.numpy as jnp
from jax import lax
from jax.sharding import PartitionSpec as P

BF16 = jnp.bfloat16
F32 = jnp.float32
GROUPS = 1
CHUNKS = 4
PIECES = 2
STREAMS = 2


def local(segments, ring, cores, layer_inputs, targets, enc_weight, enc_bias, dec_weight):
    z = lax.axis_index("feat")
    core = lax.axis_index("tok")
    segment = lax.axis_index("segment")
    odd = z % 2 == 1
    rows = layer_inputs.shape[1] // GROUPS
    width = enc_weight.shape[2] // CHUNKS
    depth = enc_weight.shape[1]
    weight = enc_weight[0]
    decoders = dec_weight[0]
    layers = decoders.shape[0]
    per_core = ring // cores

    units = [(group, chunk) for group in range(GROUPS) for chunk in range(CHUNKS)]
    finished = {}
    decoded = {}
    waiting = []
    ordered = [None]
    left = {group: CHUNKS * layers for group in range(GROUPS)}
    totals = {}
    residuals = {}

    def after(values, others):
        others = [x for x in jax.tree.leaves(others) if x is not None]
        return lax.optimization_barrier((values, others))[0] if others else values

    def background(sent):
        ordered[0] = sent
        for _ in range(min(PIECES, len(waiting))):
            ordered[0] = sent = waiting.pop(0)(sent)

    swaps = ring & (ring - 1) == 0

    def exchanged():
        places = [(i, c) for i in range(ring) for c in range(cores)]
        holds = core == z // per_core
        parts = []
        for k in range(ring):
            to = z ^ k if swaps else (z + k) % ring
            part = lax.dynamic_slice_in_dim(layer_inputs[0], (to % per_core) * depth, depth, axis=1)
            if k:
                pairs = [((i, c), (i ^ k if swaps else (i + k) % ring, c)) for i, c in places]
                pairs = [(p[0] * cores + p[1], q[0] * cores + q[1]) for p, q in pairs if q[0] // per_core == q[1]]
                part = lax.ppermute(part, ("feat", "tok"), pairs)
            else:
                part = jnp.where(holds, part, 0)
            parts.append(part)
        parts = jnp.stack(parts)
        given = parts
        for k in range(1, cores):
            pairs = [(i * cores + i // per_core, i * cores + (i // per_core + k) % cores) for i in range(ring)]
            parts += lax.ppermute(given, ("feat", "tok"), pairs)
        order = [z ^ ((z - k) % ring) if swaps else k for k in range(ring)]
        return jnp.concatenate(
            [lax.dynamic_index_in_dim(parts, i, axis=0, keepdims=False) for i in order], axis=0
        )

    columns = [exchanged()]

    def partial_sums(group, chunk):
        part = jnp.dot(
            after(columns[group], ordered), weight[:, chunk * width : (chunk + 1) * width], preferred_element_type=F32
        )
        return [part[k * rows : (k + 1) * rows] for k in range(ring)]

    def decode(unit, codes):
        group, chunk = unit

        def piece(layer):
            def run(sent):
                all_codes = after(codes_of[0], sent)
                out = lax.dot_general(
                    all_codes,
                    decoders[layer, :, chunk * width : (chunk + 1) * width],
                    (((1,), (1,)), ((), ())),
                    preferred_element_type=F32,
                )
                key = group, layer
                decoded[key] = out if key not in decoded else decoded[key] + out
                left[group] -= 1
                if not left[group]:
                    waiting.extend([lambda sent: share_cores(group, sent), lambda sent: share_segments(group, sent)])
                return decoded[key]

            return run

        codes_of = [jnp.concatenate(codes, axis=0)]
        waiting.extend(piece(layer) for layer in reversed(range(layers)))

    class Stream:
        def __init__(self, own):
            self.own = own
            self.step = 0
            self.slot = 1
            self.got = [{}, {}]
            self.sums = None

        def swap(self, value, side):
            i, k, n = self.step, self.slot, len(self.own)
            pairs = []
            for p in range(side, ring - 1, 2):
                q = ring - 2 - p
                if not (i == 0 and p >= k or i == n and p < k):
                    pairs.append((p, p + 1))
                if not (i == 0 and q >= k or i == n and q < k):
                    pairs.append((p + 1, p))
            return lax.ppermute(value, "feat", pairs) if pairs else None

        def advance(self):
            i, k, n = self.step, self.slot, len(self.own)
            if self.sums is None:
                self.sums = partial_sums(*self.own[0])
            sent = []
            for side in range(2):
                if k == 0:
                    sent.append(finished[self.own[i - 1]])
                    continue
                value = self.got[1 - side].get(k - 1)
                if value is not None:
                    value = after(value, ordered)
                if i < n:
                    rightward = odd == (side == 1)
                    own = jnp.where(
                        rightward,
                        jnp.where(k > z, self.sums[k], 0.0),
                        jnp.where(k > ring - 1 - z, self.sums[ring - k], 0.0),
                    )
                    value = (own if value is None else own + value.astype(F32)).astype(BF16)
                sent.append(value)
            for side in range(2):
                got = self.swap(sent[side], side) if sent[side] is not None else None
                if got is not None:
                    self.got[side][k] = got
            background(sent)
            if i and k == ring - 2:
                unit = self.own[i - 1]
                codes = [finished[unit]]
                zero = jnp.zeros_like(codes[0])
                for m in range(1, ring):
                    a, b = m - 1, ring - m - 1
                    left = jnp.where(odd, self.got[0].get(a, zero), self.got[1].get(a, zero))
                    right = jnp.where(odd, self.got[1].get(b, zero), self.got[0].get(b, zero))
                    codes.append(jnp.where(m <= z, left, right))
                decode(unit, codes)
            self.slot += 1
            if i < n and k == ring - 1:
                chunk = self.own[i][1]
                bias = enc_bias[0, chunk * width : (chunk + 1) * width][None, :]
                total = self.sums[0] + self.got[0][k].astype(F32) + self.got[1][k].astype(F32)
                finished[self.own[i]] = jax.nn.relu(total + bias).astype(BF16)
                self.slot, self.step = 0, i + 1
                if i + 1 < n:
                    self.sums = partial_sums(*self.own[i + 1])
                self.got = [{}, {}]
                return True
            return not (i == n and k == ring - 2)

    def share_cores(group, sent):
        blocks = after([decoded[group, layer] for layer in range(layers)], sent)
        blocks = jnp.stack(blocks).reshape(layers, ring, rows, depth)

        def share(index):
            first = index * per_core
            return jnp.stack(
                [
                    lax.dynamic_index_in_dim(blocks, (z - first - b) % ring, axis=1, keepdims=False)
                    for b in range(per_core)
                ],
                axis=1,
            )

        total = share(core)
        given = []
        for k in range(1, cores):
            given.append(share((core + k) % cores).astype(BF16))
            got = lax.ppermute(given[-1], "tok", [(i, (i + k) % cores) for i in range(cores)])
            total += got.astype(F32)
        totals[group] = total
        return given

    def share_segments(group, sent):
        total = after(totals[group], sent)
        own = lax.dynamic_index_in_dim(total, segment, axis=0, keepdims=False)
        given = []
        paired = segments & (segments - 1) == 0
        for k in range(1, segments):
            place = segment ^ k if paired else jnp.minimum(segment + k, layers - 1)
            given.append(lax.dynamic_index_in_dim(total, place, axis=0, keepdims=False).astype(BF16))
            pairs = [(i, i ^ k if paired else i + k) for i in range(segments)]
            got = lax.ppermute(given[-1], "segment", [(i, j) for i, j in pairs if i < j < segments])
            own += got.astype(F32)
        residuals[group] = own
        return given

    streams = [Stream(units[i::STREAMS]) for i in range(STREAMS)]
    going = [True] * STREAMS
    while any(going):
        for i, stream in enumerate(streams):
            if going[i]:
                going[i] = stream.advance()
    while waiting:
        background(None)
    own = jnp.stack([residuals[group] for group in range(GROUPS)], axis=1)
    residual = targets[0].astype(F32) - own.reshape(targets.shape[1:])
    features = jnp.concatenate(
        [
            jnp.concatenate([finished[group, chunk] for chunk in range(CHUNKS)], axis=1)
            for group in range(GROUPS)
        ],
        axis=0,
    )
    return (features[None], residual[None])


def solution(mesh):
    in_specs = (
        P("segment", "feat", "tok"),
        P("segment", "tok", "feat"),
        P("segment", "feat", "tok"),
        P("segment", "tok"),
        P("segment", None, "feat", "tok"),
    )
    out_specs = (P("segment", "feat", "tok"), P("segment", "tok", "feat"))
    sizes = (mesh.shape["segment"], mesh.shape["feat"], mesh.shape["tok"])
    return jax.shard_map(
        lambda *args: local(*sizes, *args), mesh=mesh, in_specs=in_specs, out_specs=out_specs, check_vma=False
    )
```

```python
import jax
import jax.numpy as jnp
from jax import lax
from jax.sharding import PartitionSpec as P

BF16 = jnp.bfloat16
F32 = jnp.float32
GROUPS = 2
CHUNKS = 2
STREAMS = 2
PIECES = 2


def local(segments, ring, cores, layer_inputs, targets, enc_weight, enc_bias, dec_weight):
    z = lax.axis_index("feat")
    core = lax.axis_index("tok")
    segment = lax.axis_index("segment")
    odd = z % 2 == 1
    rows = layer_inputs.shape[1] // GROUPS
    width = enc_weight.shape[2] // CHUNKS
    depth = enc_weight.shape[1]
    weight = enc_weight[0]
    decoders = dec_weight[0]
    layers = decoders.shape[0]
    per_core = ring // cores

    own_rows = lax.all_gather(layer_inputs[0], "tok", axis=1, tiled=True)

    swaps = ring & (ring - 1) == 0

    def exchanged(group):
        block = own_rows[group * rows : (group + 1) * rows]
        parts = []
        for k in range(ring):
            to = z ^ k if swaps else (z + k) % ring
            part = lax.dynamic_slice_in_dim(block, to * depth, depth, axis=1)
            if k:
                pairs = [(i, i ^ k if swaps else (i + k) % ring) for i in range(ring)]
                part = lax.ppermute(part, "feat", pairs)
            parts.append(part)
        if swaps:
            both = jnp.stack(parts)
            parts = [
                lax.dynamic_index_in_dim(both, z ^ ((z - k) % ring), axis=0, keepdims=False) for k in range(ring)
            ]
        return jnp.concatenate(parts, axis=0)

    columns = [exchanged(group) for group in range(GROUPS)]

    def partial_sums(group, chunk):
        part = jnp.dot(
            columns[group], weight[:, chunk * width : (chunk + 1) * width], preferred_element_type=F32
        )
        return [part[k * rows : (k + 1) * rows] for k in range(ring)]

    units = [(group, chunk) for group in range(GROUPS) for chunk in range(CHUNKS)]
    finished = {}
    decoded = {}
    waiting = []
    ordered = [None]
    left = {g: [(c, t) for c in range(CHUNKS) for t in range(layers)] for g in range(GROUPS)}
    totals = {}
    residuals = {}

    def after(values, others):
        others = [x for x in jax.tree.leaves(others) if x is not None]
        return lax.optimization_barrier((values, others))[0] if others else values

    def background(sent):
        for _ in range(PIECES):
            if waiting:
                work, alone = waiting.pop(0)
                ordered[0] = sent = work(sent)
                if alone:
                    break

    def decode(unit, codes):
        group, chunk = unit

        def piece(layer):
            def run(sent):
                all_codes = after(codes_of[0], [sent, residuals.get(group - 1)])
                out = lax.dot_general(
                    all_codes,
                    decoders[layer, :, chunk * width : (chunk + 1) * width],
                    (((1,), (1,)), ((), ())),
                    preferred_element_type=F32,
                )
                key = group, layer
                decoded[key] = out if key not in decoded else decoded[key] + out
                left[group].remove((chunk, layer))
                if not left[group]:
                    waiting.append((lambda sent: share_segments(group, sent), True))
                elif all(other == 0 for _, other in left[group]) and layer:
                    waiting.insert(0, (lambda sent: share_cores(group, sent), True))
                return decoded[key]

            return run

        codes_of = [jnp.concatenate(codes, axis=0)]
        waiting.extend((piece(layer), False) for layer in reversed(range(layers)))

    class Stream:
        def __init__(self, own):
            self.own = own
            self.step = 0
            self.slot = 1
            self.got = [{}, {}]
            self.sums = partial_sums(*own[0])

        def swap(self, value, side):
            i, k, n = self.step, self.slot, len(self.own)
            pairs = []
            for p in range(side, ring - 1, 2):
                q = ring - 2 - p
                if not (i == 0 and p >= k or i == n and p < k):
                    pairs.append((p, p + 1))
                if not (i == 0 and q >= k or i == n and q < k):
                    pairs.append((p + 1, p))
            return lax.ppermute(value, "feat", pairs) if pairs else None

        def advance(self):
            i, k, n = self.step, self.slot, len(self.own)
            sent = []
            for side in range(2):
                if k == 0:
                    sent.append(finished[self.own[i - 1]])
                    continue
                value = self.got[1 - side].get(k - 1)
                if value is not None:
                    value = after(value, ordered)
                if i < n:
                    rightward = odd == (side == 1)
                    own = jnp.where(
                        rightward,
                        jnp.where(k > z, self.sums[k], 0.0),
                        jnp.where(k > ring - 1 - z, self.sums[ring - k], 0.0),
                    )
                    value = (own if value is None else own + value.astype(F32)).astype(BF16)
                sent.append(value)
            for side in range(2):
                got = self.swap(sent[side], side) if sent[side] is not None else None
                if got is not None:
                    self.got[side][k] = got
            background(sent)
            if i and k == ring - 2:
                unit = self.own[i - 1]
                codes = [finished[unit]]
                zero = jnp.zeros_like(codes[0])
                for m in range(1, ring):
                    a, b = m - 1, ring - m - 1
                    left = jnp.where(odd, self.got[0].get(a, zero), self.got[1].get(a, zero))
                    right = jnp.where(odd, self.got[1].get(b, zero), self.got[0].get(b, zero))
                    codes.append(jnp.where(m <= z, left, right))
                decode(unit, codes)
            self.slot += 1
            if i < n and k == ring - 1:
                chunk = self.own[i][1]
                bias = enc_bias[0, chunk * width : (chunk + 1) * width][None, :]
                total = self.sums[0] + self.got[0][k].astype(F32) + self.got[1][k].astype(F32)
                finished[self.own[i]] = jax.nn.relu(total + bias).astype(BF16)
                self.slot, self.step = 0, i + 1
                if i + 1 < n:
                    self.sums = partial_sums(*self.own[i + 1])
                self.got = [{}, {}]
                return True
            return not (i == n and k == ring - 2)

    def share_cores(group, sent, first=1):
        blocks = after([decoded[group, layer] for layer in range(first, layers if first else 1)], sent)
        blocks = jnp.stack(blocks).reshape(-1, ring, rows, depth)

        def share(index):
            begin = index * per_core
            return jnp.stack(
                [
                    lax.dynamic_index_in_dim(blocks, (z - begin - b) % ring, axis=1, keepdims=False)
                    for b in range(per_core)
                ],
                axis=1,
            )

        total = share(core)
        given = []
        for k in range(1, cores):
            given.append(share((core + k) % cores).astype(BF16))
            got = lax.ppermute(given[-1], "tok", [(i, (i + k) % cores) for i in range(cores)])
            total += got.astype(F32)
        totals[group, first] = total
        return given

    def share_segments(group, sent):
        total = after(totals[group, 1], sent)
        paired = segments & (segments - 1) == 0
        received, given = [], []
        for k in range(1, segments):
            place = segment ^ k if paired else jnp.minimum(segment + k, layers - 1)
            given.append(lax.dynamic_index_in_dim(total, jnp.maximum(place, 1) - 1, axis=0, keepdims=False).astype(BF16))
            pairs = [(i, i ^ k if paired else i + k) for i in range(segments)]
            got = lax.ppermute(given[-1], "segment", [(i, j) for i, j in pairs if i < j < segments])
            received.append(got)
        share_cores(group, given, 0)
        own = jnp.where(
            segment == 0,
            totals[group, 0][0],
            lax.dynamic_index_in_dim(total, jnp.maximum(segment, 1) - 1, axis=0, keepdims=False),
        )
        residuals[group] = sum([got.astype(F32) for got in received], own)
        return given

    streams = [Stream(units[i::STREAMS]) for i in range(STREAMS)]
    going = [True] * STREAMS
    while any(going):
        for i, stream in enumerate(streams):
            if going[i]:
                going[i] = stream.advance()
    while waiting:
        background(None)
    own = jnp.stack([residuals[group] for group in range(GROUPS)], axis=1)
    residual = targets[0].astype(F32) - own.reshape(targets.shape[1:])
    features = jnp.concatenate(
        [
            jnp.concatenate([finished[group, chunk] for chunk in range(CHUNKS)], axis=1)
            for group in range(GROUPS)
        ],
        axis=0,
    )
    return (features[None], residual[None])


def solution(mesh):
    in_specs = (
        P("segment", "feat", "tok"),
        P("segment", "tok", "feat"),
        P("segment", "feat", "tok"),
        P("segment", "tok"),
        P("segment", None, "feat", "tok"),
    )
    out_specs = (P("segment", "feat", "tok"), P("segment", "tok", "feat"))
    sizes = (mesh.shape["segment"], mesh.shape["feat"], mesh.shape["tok"])
    return jax.shard_map(
        lambda *args: local(*sizes, *args), mesh=mesh, in_specs=in_specs, out_specs=out_specs, check_vma=False
    )
```

```python
import jax
import jax.numpy as jnp
from jax import lax
from jax.sharding import PartitionSpec as P

BF16 = jnp.bfloat16
F32 = jnp.float32
GROUPS = 2
CHUNKS = 2
STREAMS = 2
PIECES = 2


def local(segments, ring, cores, layer_inputs, targets, enc_weight, enc_bias, dec_weight):
    z = lax.axis_index("feat")
    core = lax.axis_index("tok")
    segment = lax.axis_index("segment")
    odd = z % 2 == 1
    rows = layer_inputs.shape[1] // GROUPS
    width = enc_weight.shape[2] // CHUNKS
    depth = enc_weight.shape[1]
    weight = enc_weight[0]
    decoders = dec_weight[0]
    layers = decoders.shape[0]
    per_core = ring // cores

    own_rows = lax.all_gather(layer_inputs[0], "tok", axis=1, tiled=True)

    swaps = ring & (ring - 1) == 0

    def exchanged():
        share = own_rows.shape[0] // cores
        block = lax.dynamic_slice_in_dim(own_rows, core * share, share, axis=0)
        parts = []
        for k in range(ring):
            to = z ^ k if swaps else (z + k) % ring
            part = lax.dynamic_slice_in_dim(block, to * depth, depth, axis=1)
            if k:
                pairs = [(i, i ^ k if swaps else (i + k) % ring) for i in range(ring)]
                part = lax.ppermute(part, "feat", pairs)
            parts.append(part)
        every = lax.all_gather(jnp.stack(parts), "tok", axis=1, tiled=True)
        order = [z ^ ((z - k) % ring) if swaps else k for k in range(ring)]
        every = [lax.dynamic_index_in_dim(every, i, axis=0, keepdims=False) for i in order]
        return [
            jnp.concatenate([part[group * rows : (group + 1) * rows] for part in every], axis=0)
            for group in range(GROUPS)
        ]

    columns = exchanged()

    def partial_sums(group, chunk):
        part = jnp.dot(
            columns[group], weight[:, chunk * width : (chunk + 1) * width], preferred_element_type=F32
        )
        return [part[k * rows : (k + 1) * rows] for k in range(ring)]

    units = [(group, chunk) for group in range(GROUPS) for chunk in range(CHUNKS)]
    finished = {}
    decoded = {}
    waiting = []
    ordered = [None]
    left = {g: [(c, t) for c in range(CHUNKS) for t in range(layers)] for g in range(GROUPS)}
    totals = {}
    residuals = {}

    def after(values, others):
        others = [x for x in jax.tree.leaves(others) if x is not None]
        return lax.optimization_barrier((values, others))[0] if others else values

    def background(sent):
        for _ in range(PIECES):
            if waiting:
                work, alone = waiting.pop(0)
                ordered[0] = sent = work(sent)
                if alone:
                    break

    def decode(unit, codes):
        group, chunk = unit

        def piece(layer):
            def run(sent):
                all_codes = after(codes_of[0], sent)
                out = lax.dot_general(
                    all_codes,
                    decoders[layer, :, chunk * width : (chunk + 1) * width],
                    (((1,), (1,)), ((), ())),
                    preferred_element_type=F32,
                )
                key = group, layer
                decoded[key] = out if key not in decoded else decoded[key] + out
                left[group].remove((chunk, layer))
                if group < GROUPS - 1:
                    if not left[group]:
                        waiting.extend([(lambda sent: scatter_cores(group, sent), True), (wait, True)])
                        waiting.append((lambda sent: scatter_segments(group, sent), True))
                elif not left[group]:
                    waiting.append((lambda sent: share_segments(group, sent), True))
                elif all(other == 0 for _, other in left[group]) and layer:
                    waiting.insert(0, (lambda sent: share_cores(group, sent), True))
                return decoded[key]

            return run

        codes_of = [jnp.concatenate(codes, axis=0)]
        waiting.extend((piece(layer), False) for layer in reversed(range(layers)))

    class Stream:
        def __init__(self, own):
            self.own = own
            self.step = 0
            self.slot = 1
            self.got = [{}, {}]
            self.sums = partial_sums(*own[0])

        def swap(self, value, side):
            i, k, n = self.step, self.slot, len(self.own)
            pairs = []
            for p in range(side, ring - 1, 2):
                q = ring - 2 - p
                if not (i == 0 and p >= k or i == n and p < k):
                    pairs.append((p, p + 1))
                if not (i == 0 and q >= k or i == n and q < k):
                    pairs.append((p + 1, p))
            return lax.ppermute(value, "feat", pairs) if pairs else None

        def advance(self):
            i, k, n = self.step, self.slot, len(self.own)
            sent = []
            for side in range(2):
                if k == 0:
                    sent.append(finished[self.own[i - 1]])
                    continue
                value = self.got[1 - side].get(k - 1)
                if value is not None:
                    value = after(value, ordered)
                if i < n:
                    rightward = odd == (side == 1)
                    own = jnp.where(
                        rightward,
                        jnp.where(k > z, self.sums[k], 0.0),
                        jnp.where(k > ring - 1 - z, self.sums[ring - k], 0.0),
                    )
                    value = (own if value is None else own + value.astype(F32)).astype(BF16)
                sent.append(value)
            for side in range(2):
                got = self.swap(sent[side], side) if sent[side] is not None else None
                if got is not None:
                    self.got[side][k] = got
            background(sent)
            if i and k == ring - 2:
                unit = self.own[i - 1]
                codes = [finished[unit]]
                zero = jnp.zeros_like(codes[0])
                for m in range(1, ring):
                    a, b = m - 1, ring - m - 1
                    left = jnp.where(odd, self.got[0].get(a, zero), self.got[1].get(a, zero))
                    right = jnp.where(odd, self.got[1].get(b, zero), self.got[0].get(b, zero))
                    codes.append(jnp.where(m <= z, left, right))
                decode(unit, codes)
            self.slot += 1
            if i < n and k == ring - 1:
                chunk = self.own[i][1]
                bias = enc_bias[0, chunk * width : (chunk + 1) * width][None, :]
                total = self.sums[0] + self.got[0][k].astype(F32) + self.got[1][k].astype(F32)
                finished[self.own[i]] = jax.nn.relu(total + bias).astype(BF16)
                self.slot, self.step = 0, i + 1
                if i + 1 < n:
                    self.sums = partial_sums(*self.own[i + 1])
                self.got = [{}, {}]
                return True
            return not (i == n and k == ring - 2)

    def wait(sent):
        return sent

    def scatter_cores(group, sent):
        blocks = after([decoded[group, layer] for layer in range(layers)], sent)
        blocks = jnp.stack([jnp.where(layer >= segment, blocks[layer], 0.0) for layer in range(layers)])
        blocks = blocks.astype(BF16).reshape(layers, ring, rows, depth)
        blocks = jnp.stack(
            [lax.dynamic_index_in_dim(blocks, (z - b) % ring, axis=1, keepdims=False) for b in range(ring)], axis=1
        )
        totals[group] = lax.psum_scatter(blocks, "tok", scatter_dimension=1, tiled=True)
        return blocks

    def scatter_segments(group, sent):
        total = after(totals[group], sent)
        residuals[group] = lax.psum_scatter(total, "segment", scatter_dimension=0, tiled=True)[0].astype(F32)
        return total

    def share_cores(group, sent, first=1):
        blocks = after([decoded[group, layer] for layer in range(first, layers if first else 1)], sent)
        blocks = jnp.stack(blocks).reshape(-1, ring, rows, depth)

        def share(index):
            begin = index * per_core
            return jnp.stack(
                [
                    lax.dynamic_index_in_dim(blocks, (z - begin - b) % ring, axis=1, keepdims=False)
                    for b in range(per_core)
                ],
                axis=1,
            )

        total = share(core)
        given = []
        for k in range(1, cores):
            given.append(share((core + k) % cores).astype(BF16))
            got = lax.ppermute(given[-1], "tok", [(i, (i + k) % cores) for i in range(cores)])
            total += got.astype(F32)
        totals[group, first] = total
        return given

    def share_segments(group, sent):
        total = after(totals[group, 1], sent)
        paired = segments & (segments - 1) == 0
        received, given = [], []
        for k in range(1, segments):
            place = segment ^ k if paired else jnp.minimum(segment + k, layers - 1)
            given.append(lax.dynamic_index_in_dim(total, jnp.maximum(place, 1) - 1, axis=0, keepdims=False).astype(BF16))
            pairs = [(i, i ^ k if paired else i + k) for i in range(segments)]
            got = lax.ppermute(given[-1], "segment", [(i, j) for i, j in pairs if i < j < segments])
            received.append(got)
        share_cores(group, given, 0)
        own = jnp.where(
            segment == 0,
            totals[group, 0][0],
            lax.dynamic_index_in_dim(total, jnp.maximum(segment, 1) - 1, axis=0, keepdims=False),
        )
        residuals[group] = sum([got.astype(F32) for got in received], own)
        return given

    streams = [Stream(units[i::STREAMS]) for i in range(STREAMS)]
    going = [True] * STREAMS
    while any(going):
        for i, stream in enumerate(streams):
            if going[i]:
                going[i] = stream.advance()
    while waiting:
        background(None)
    own = jnp.stack([residuals[group] for group in range(GROUPS)], axis=1)
    residual = targets[0].astype(F32) - own.reshape(targets.shape[1:])
    features = jnp.concatenate(
        [
            jnp.concatenate([finished[group, chunk] for chunk in range(CHUNKS)], axis=1)
            for group in range(GROUPS)
        ],
        axis=0,
    )
    return (features[None], residual[None])


def solution(mesh):
    in_specs = (
        P("segment", "feat", "tok"),
        P("segment", "tok", "feat"),
        P("segment", "feat", "tok"),
        P("segment", "tok"),
        P("segment", None, "feat", "tok"),
    )
    out_specs = (P("segment", "feat", "tok"), P("segment", "tok", "feat"))
    sizes = (mesh.shape["segment"], mesh.shape["feat"], mesh.shape["tok"])
    return jax.shard_map(
        lambda *args: local(*sizes, *args), mesh=mesh, in_specs=in_specs, out_specs=out_specs, check_vma=False
    )
```

```python
import jax
import jax.numpy as jnp
from jax import lax
from jax.experimental import pallas as pl
from jax.experimental.pallas import tpu as pltpu
from jax.sharding import PartitionSpec as P

BF16 = jnp.bfloat16
F32 = jnp.float32
GROUPS = 2
CHUNKS = 2
STREAMS = 2


def decode_targets(codes, dec_weight, earlier, first, targets, chunk):
    tokens, width = codes.shape
    depth = dec_weight.shape[2]
    steps = width // 1024 if width % 1024 == 0 else 1
    block = width // steps

    def kernel(codes_ref, weight_ref, *refs):
        out_ref = refs[-1]
        product = lax.dot_general(
            codes_ref[...], weight_ref[...], (((1,), (1,)), ((), ())), preferred_element_type=F32
        )

        @pl.when(pl.program_id(1) == 0)
        def _():
            out_ref[...] = product if earlier is None else refs[0][...] + product

        @pl.when(pl.program_id(1) > 0)
        def _():
            out_ref[...] += product

    total = pl.BlockSpec((None, tokens, depth), lambda t, k: (t, 0, 0))
    given = [] if earlier is None else [earlier]
    return pl.pallas_call(
        kernel,
        grid=(targets, steps),
        in_specs=[
            pl.BlockSpec((tokens, block), lambda t, k: (0, k)),
            pl.BlockSpec((None, None, depth, block), lambda t, k: (0, first + t, 0, chunk * steps + k)),
        ]
        + [total] * len(given),
        out_specs=total,
        out_shape=jax.ShapeDtypeStruct((targets, tokens, depth), F32),
        compiler_params=pltpu.CompilerParams(vmem_limit_bytes=20 * 1024 * 1024),
        cost_estimate=pl.CostEstimate(
            flops=2 * targets * tokens * width * depth,
            bytes_accessed=2 * targets * width * depth + 8 * targets * tokens * depth,
            transcendentals=0,
        ),
    )(codes, dec_weight, *given)


def local(segments, ring, cores, layer_inputs, targets, enc_weight, enc_bias, dec_weight):
    z = lax.axis_index("feat")
    core = lax.axis_index("tok")
    segment = lax.axis_index("segment")
    odd = z % 2 == 1
    rows = layer_inputs.shape[1] // GROUPS
    width = enc_weight.shape[2] // CHUNKS
    depth = enc_weight.shape[1]
    weight = enc_weight[0]
    decoders = dec_weight[0]
    layers = decoders.shape[0]
    per_core = ring // cores

    own_rows = lax.all_gather(layer_inputs[0], "tok", axis=1, tiled=True)

    swaps = ring & (ring - 1) == 0

    def exchanged():
        share = own_rows.shape[0] // cores
        block = lax.dynamic_slice_in_dim(own_rows, core * share, share, axis=0)
        parts = []
        for k in range(ring):
            to = z ^ k if swaps else (z + k) % ring
            part = lax.dynamic_slice_in_dim(block, to * depth, depth, axis=1)
            if k:
                pairs = [(i, i ^ k if swaps else (i + k) % ring) for i in range(ring)]
                part = lax.ppermute(part, "feat", pairs)
            parts.append(part)
        every = lax.all_gather(jnp.stack(parts), "tok", axis=1, tiled=True)
        order = [z ^ ((z - k) % ring) if swaps else k for k in range(ring)]
        every = [lax.dynamic_index_in_dim(every, i, axis=0, keepdims=False) for i in order]
        return [
            jnp.concatenate([part[group * rows : (group + 1) * rows] for part in every], axis=0)
            for group in range(GROUPS)
        ]

    columns = exchanged()

    def partial_sums(group, chunk):
        part = jnp.dot(
            columns[group], weight[:, chunk * width : (chunk + 1) * width], preferred_element_type=F32
        )
        return [part[k * rows : (k + 1) * rows] for k in range(ring)]

    units = [(group, chunk) for group in range(GROUPS) for chunk in range(CHUNKS)]
    finished = {}
    decoded = {}
    waiting = []
    ordered = [None]
    low = []
    totals = {}
    residuals = {}

    def after(values, others):
        others = [x for x in jax.tree.leaves(others) if x is not None]
        return lax.optimization_barrier((values, others))[0] if others else values

    def background(sent):
        if waiting:
            ordered[0] = waiting.pop(0)(sent)

    def decode(unit, codes):
        group, chunk = unit
        all_codes = jnp.concatenate(codes, axis=0)

        def piece(first, targets):
            def run(sent):
                key = group, first
                decoded[key] = decode_targets(
                    after(all_codes, sent), dec_weight, decoded.get(key), first, targets, chunk
                )
                return decoded[key]

            return run

        waiting.append(piece(1, layers - 1))
        (low if group == GROUPS - 1 else waiting).append(piece(0, 1))

    class Stream:
        def __init__(self, own):
            self.own = own
            self.step = 0
            self.slot = 1
            self.got = [{}, {}]
            self.sums = partial_sums(*own[0])

        def swap(self, value, side):
            i, k, n = self.step, self.slot, len(self.own)
            pairs = []
            for p in range(side, ring - 1, 2):
                q = ring - 2 - p
                if not (i == 0 and p >= k or i == n and p < k):
                    pairs.append((p, p + 1))
                if not (i == 0 and q >= k or i == n and q < k):
                    pairs.append((p + 1, p))
            return lax.ppermute(value, "feat", pairs) if pairs else None

        def advance(self):
            i, k, n = self.step, self.slot, len(self.own)
            sent = []
            for side in range(2):
                if k == 0:
                    sent.append(finished[self.own[i - 1]])
                    continue
                value = self.got[1 - side].get(k - 1)
                if value is not None:
                    value = after(value, ordered)
                if i < n:
                    rightward = odd == (side == 1)
                    own = jnp.where(
                        rightward,
                        jnp.where(k > z, self.sums[k], 0.0),
                        jnp.where(k > ring - 1 - z, self.sums[ring - k], 0.0),
                    )
                    value = (own if value is None else own + value.astype(F32)).astype(BF16)
                sent.append(value)
            for side in range(2):
                got = self.swap(sent[side], side) if sent[side] is not None else None
                if got is not None:
                    self.got[side][k] = got
            if i < n or k < ring - 2:
                background(sent)
            if i and k == ring - 2:
                unit = self.own[i - 1]
                codes = [finished[unit]]
                zero = jnp.zeros_like(codes[0])
                for m in range(1, ring):
                    a, b = m - 1, ring - m - 1
                    left = jnp.where(odd, self.got[0].get(a, zero), self.got[1].get(a, zero))
                    right = jnp.where(odd, self.got[1].get(b, zero), self.got[0].get(b, zero))
                    codes.append(jnp.where(m <= z, left, right))
                decode(unit, codes)
            self.slot += 1
            self.sent = sent
            if i < n and k == ring - 1:
                chunk = self.own[i][1]
                bias = enc_bias[0, chunk * width : (chunk + 1) * width][None, :]
                total = self.sums[0] + self.got[0][k].astype(F32) + self.got[1][k].astype(F32)
                finished[self.own[i]] = jax.nn.relu(total + bias).astype(BF16)
                self.slot, self.step = 0, i + 1
                if i + 1 < n:
                    self.sums = partial_sums(*self.own[i + 1])
                self.got = [{}, {}]
                return True
            return not (i == n and k == ring - 2)

    def share_cores(group, sent, first=1):
        blocks = after(decoded[group, first], sent).reshape(-1, ring, rows, depth)

        def share(index):
            begin = index * per_core
            return jnp.stack(
                [
                    lax.dynamic_index_in_dim(blocks, (z - begin - b) % ring, axis=1, keepdims=False)
                    for b in range(per_core)
                ],
                axis=1,
            )

        total = share(core)
        given = []
        for k in range(1, cores):
            given.append(share((core + k) % cores).astype(BF16))
            got = lax.ppermute(given[-1], "tok", [(i, (i + k) % cores) for i in range(cores)])
            total += got.astype(F32)
        totals[group, first] = total
        return given

    def share_segments(group, sent):
        total = after(totals[group, 1], sent)
        paired = segments & (segments - 1) == 0
        received, given = [], []
        for k in range(1, segments):
            place = segment ^ k if paired else jnp.minimum(segment + k, layers - 1)
            given.append(lax.dynamic_index_in_dim(total, jnp.maximum(place, 1) - 1, axis=0, keepdims=False).astype(BF16))
            pairs = [(i, i ^ k if paired else i + k) for i in range(segments)]
            got = lax.ppermute(given[-1], "segment", [(i, j) for i, j in pairs if i < j < segments])
            received.append(got)
        own = jnp.where(
            segment == 0,
            totals[group, 0][0],
            lax.dynamic_index_in_dim(total, jnp.maximum(segment, 1) - 1, axis=0, keepdims=False),
        )
        residuals[group] = sum([got.astype(F32) for got in received], own)
        return given

    streams = [Stream(units[i::STREAMS]) for i in range(STREAMS)]
    going = [True] * STREAMS
    while any(going):
        for i, stream in enumerate(streams):
            if going[i]:
                going[i] = stream.advance()
    sent = [stream.sent for stream in streams]
    last = waiting[-STREAMS:]
    for work in waiting[:-STREAMS]:
        sent = work(sent)
    for group in range(GROUPS - 1):
        sent = share_cores(group, sent)
        share_cores(group, sent, 0)
        sent = share_segments(group, sent)
    for work in last:
        sent = work(sent)
    sent = share_cores(GROUPS - 1, sent)
    for work in low:
        sent = work([sent, residuals.get(GROUPS - 2)])
    share_cores(GROUPS - 1, sent, 0)
    share_segments(GROUPS - 1, sent)
    own = jnp.stack([residuals[group] for group in range(GROUPS)], axis=1)
    residual = targets[0].astype(F32) - own.reshape(targets.shape[1:])
    features = jnp.concatenate(
        [
            jnp.concatenate([finished[group, chunk] for chunk in range(CHUNKS)], axis=1)
            for group in range(GROUPS)
        ],
        axis=0,
    )
    return (features[None], residual[None])


def solution(mesh):
    in_specs = (
        P("segment", "feat", "tok"),
        P("segment", "tok", "feat"),
        P("segment", "feat", "tok"),
        P("segment", "tok"),
        P("segment", None, "feat", "tok"),
    )
    out_specs = (P("segment", "feat", "tok"), P("segment", "tok", "feat"))
    sizes = (mesh.shape["segment"], mesh.shape["feat"], mesh.shape["tok"])
    return jax.shard_map(
        lambda *args: local(*sizes, *args), mesh=mesh, in_specs=in_specs, out_specs=out_specs, check_vma=False
    )
```

```python
import jax
import jax.numpy as jnp
from jax import lax
from jax.sharding import PartitionSpec as P

BF16 = jnp.bfloat16
F32 = jnp.float32
GROUPS = 2
CHUNKS = 2
STREAMS = 2
PIECES = 2


def local(segments, ring, cores, layer_inputs, targets, enc_weight, enc_bias, dec_weight):
    z = lax.axis_index("feat")
    core = lax.axis_index("tok")
    segment = lax.axis_index("segment")
    odd = z % 2 == 1
    rows = layer_inputs.shape[1] // GROUPS
    width = enc_weight.shape[2] // CHUNKS
    depth = enc_weight.shape[1]
    weight = enc_weight[0]
    decoders = dec_weight[0]
    layers = decoders.shape[0]
    per_core = ring // cores

    own_rows = lax.all_gather(layer_inputs[0], "tok", axis=1, tiled=True)

    swaps = ring & (ring - 1) == 0

    def exchanged():
        share = own_rows.shape[0] // cores
        block = lax.dynamic_slice_in_dim(own_rows, core * share, share, axis=0)
        parts = []
        for k in range(ring):
            to = z ^ k if swaps else (z + k) % ring
            part = lax.dynamic_slice_in_dim(block, to * depth, depth, axis=1)
            if k:
                pairs = [(i, i ^ k if swaps else (i + k) % ring) for i in range(ring)]
                part = lax.ppermute(part, "feat", pairs)
            parts.append(part)
        every = lax.all_gather(jnp.stack(parts), "tok", axis=1, tiled=True)
        order = [z ^ ((z - k) % ring) if swaps else k for k in range(ring)]
        every = [lax.dynamic_index_in_dim(every, i, axis=0, keepdims=False) for i in order]
        return [
            jnp.concatenate([part[group * rows : (group + 1) * rows] for part in every], axis=0)
            for group in range(GROUPS)
        ]

    columns = exchanged()

    def partial_sums(group, chunk):
        part = jnp.dot(
            columns[group], weight[:, chunk * width : (chunk + 1) * width], preferred_element_type=F32
        ).astype(BF16)
        return [part[k * rows : (k + 1) * rows] for k in range(ring)]

    units = [(group, chunk) for group in range(GROUPS) for chunk in range(CHUNKS)]
    finished = {}
    decoded = {}
    waiting = []
    ordered = [None]
    last = []
    totals = {}
    residuals = {}

    def after(values, others):
        others = [x for x in jax.tree.leaves(others) if x is not None]
        return lax.optimization_barrier((values, others))[0] if others else values

    def background(sent):
        for _ in range(min(PIECES, len(waiting))):
            ordered[0] = sent = waiting.pop(0)(sent)

    def decode(unit, own, got):
        group, chunk = unit
        codes = []

        def selected(sent):
            mine, (even, other) = after((own, got), sent)
            parts = [mine]
            zero = jnp.zeros_like(mine)
            for m in range(1, ring):
                a, b = m - 1, ring - m - 1
                left = jnp.where(odd, even.get(a, zero), other.get(a, zero))
                right = jnp.where(odd, other.get(b, zero), even.get(b, zero))
                parts.append(jnp.where(m <= z, left, right))
            return jnp.concatenate(parts, axis=0)

        def piece(layer):
            def run(sent):
                if not codes:
                    codes.append(selected(sent))
                out = lax.dot_general(
                    after(codes[0], sent),
                    decoders[layer, :, chunk * width : (chunk + 1) * width],
                    (((1,), (1,)), ((), ())),
                    preferred_element_type=F32,
                )
                key = group, layer
                decoded[key] = out if key not in decoded else decoded[key] + out
                return decoded[key]

            return run

        (waiting if group < GROUPS - 1 else last).append(piece)
        if group < GROUPS - 1:
            waiting[-1:] = [piece(layer) for layer in reversed(range(layers))]

    class Stream:
        def __init__(self, own):
            self.own = own
            self.step = 0
            self.slot = 1
            self.got = [{}, {}]
            self.sums = partial_sums(*own[0])

        def swap(self, value, side):
            i, k, n = self.step, self.slot, len(self.own)
            pairs = []
            for p in range(side, ring - 1, 2):
                q = ring - 2 - p
                if not (i == 0 and p >= k or i == n and p < k):
                    pairs.append((p, p + 1))
                if not (i == 0 and q >= k or i == n and q < k):
                    pairs.append((p + 1, p))
            return lax.ppermute(value, "feat", pairs) if pairs else None

        def advance(self):
            i, k, n = self.step, self.slot, len(self.own)
            sent = []
            for side in range(2):
                if k == 0:
                    sent.append(finished[self.own[i - 1]])
                    continue
                value = self.got[1 - side].get(k - 1)
                if value is not None:
                    value = after(value, ordered)
                if i < n:
                    rightward = odd == (side == 1)
                    zero = jnp.zeros_like(self.sums[k])
                    own = jnp.where(
                        rightward,
                        jnp.where(k > z, self.sums[k], zero),
                        jnp.where(k > ring - 1 - z, self.sums[ring - k], zero),
                    )
                    value = own if value is None else (own.astype(F32) + value.astype(F32)).astype(BF16)
                sent.append(value)
            for side in range(2):
                got = self.swap(sent[side], side) if sent[side] is not None else None
                if got is not None:
                    self.got[side][k] = got
            if i < n or k < ring - 2:
                background(sent)
            self.sent = sent
            if i and k == ring - 2:
                unit = self.own[i - 1]
                decode(unit, finished[unit], tuple(dict(got) for got in self.got))
            self.slot += 1
            if i < n and k == ring - 1:
                chunk = self.own[i][1]
                bias = enc_bias[0, chunk * width : (chunk + 1) * width][None, :]
                total = self.sums[0].astype(F32) + self.got[0][k].astype(F32) + self.got[1][k].astype(F32)
                finished[self.own[i]] = jax.nn.relu(total + bias).astype(BF16)
                self.slot, self.step = 0, i + 1
                if i + 1 < n:
                    self.sums = partial_sums(*self.own[i + 1])
                self.got = [{}, {}]
                return True
            return not (i == n and k == ring - 2)

    def share_cores(group, sent, first=1):
        blocks = after([decoded[group, layer] for layer in range(first, layers if first else 1)], sent)
        blocks = jnp.stack(blocks).reshape(-1, ring, rows, depth)

        def share(index):
            begin = index * per_core
            return jnp.stack(
                [
                    lax.dynamic_index_in_dim(blocks, (z - begin - b) % ring, axis=1, keepdims=False)
                    for b in range(per_core)
                ],
                axis=1,
            )

        total = share(core)
        given = []
        for k in range(1, cores):
            given.append(share((core + k) % cores).astype(BF16))
            got = lax.ppermute(given[-1], "tok", [(i, (i + k) % cores) for i in range(cores)])
            total += got.astype(F32)
        totals[group, first] = total
        return given

    def share_segments(group, sent):
        total = after(totals[group, 1], sent)
        paired = segments & (segments - 1) == 0
        received, given = [], []
        for k in range(1, segments):
            place = segment ^ k if paired else jnp.minimum(segment + k, layers - 1)
            given.append(lax.dynamic_index_in_dim(total, jnp.maximum(place, 1) - 1, axis=0, keepdims=False).astype(BF16))
            pairs = [(i, i ^ k if paired else i + k) for i in range(segments)]
            got = lax.ppermute(given[-1], "segment", [(i, j) for i, j in pairs if i < j < segments])
            received.append(got)
        own = jnp.where(
            segment == 0,
            totals[group, 0][0],
            lax.dynamic_index_in_dim(total, jnp.maximum(segment, 1) - 1, axis=0, keepdims=False),
        )
        residuals[group] = sum([got.astype(F32) for got in received], own)
        return given

    streams = [Stream(units[i::STREAMS]) for i in range(STREAMS)]
    going = [True] * STREAMS
    while any(going):
        for i, stream in enumerate(streams):
            if going[i]:
                going[i] = stream.advance()
    sent = [stream.sent for stream in streams]
    for work in waiting:
        sent = work(sent)
    for group in range(GROUPS - 1):
        sent = share_cores(group, sent)
        share_cores(group, sent, 0)
        sent = share_segments(group, sent)
    for layer in reversed(range(layers)):
        for piece in last:
            sent = piece(layer)([sent, residuals.get(GROUPS - 2)] if layer == 0 else sent)
        if layer == 1:
            sent = share_cores(GROUPS - 1, sent)
    share_cores(GROUPS - 1, sent, 0)
    share_segments(GROUPS - 1, sent)
    own = jnp.stack([residuals[group] for group in range(GROUPS)], axis=1)
    residual = targets[0].astype(F32) - own.reshape(targets.shape[1:])
    features = jnp.concatenate(
        [
            jnp.concatenate([finished[group, chunk] for chunk in range(CHUNKS)], axis=1)
            for group in range(GROUPS)
        ],
        axis=0,
    )
    return (features[None], residual[None])


def solution(mesh):
    in_specs = (
        P("segment", "feat", "tok"),
        P("segment", "tok", "feat"),
        P("segment", "feat", "tok"),
        P("segment", "tok"),
        P("segment", None, "feat", "tok"),
    )
    out_specs = (P("segment", "feat", "tok"), P("segment", "tok", "feat"))
    sizes = (mesh.shape["segment"], mesh.shape["feat"], mesh.shape["tok"])
    return jax.shard_map(
        lambda *args: local(*sizes, *args), mesh=mesh, in_specs=in_specs, out_specs=out_specs, check_vma=False
    )
```

```python
import jax
import jax.numpy as jnp
from jax import lax
from jax.sharding import PartitionSpec as P

BF16 = jnp.bfloat16
F32 = jnp.float32
GROUPS = 2
CHUNKS = 2
STREAMS = 2
PIECES = 2


def local(segments, ring, cores, layer_inputs, targets, enc_weight, enc_bias, dec_weight):
    z = lax.axis_index("feat")
    core = lax.axis_index("tok")
    segment = lax.axis_index("segment")
    odd = z % 2 == 1
    rows = layer_inputs.shape[1] // GROUPS
    width = enc_weight.shape[2] // CHUNKS
    depth = enc_weight.shape[1]
    weight = enc_weight[0]
    decoders = dec_weight[0]
    layers = decoders.shape[0]
    per_core = ring // cores

    own_rows = lax.all_gather(layer_inputs[0], "tok", axis=1, tiled=True)

    swaps = ring & (ring - 1) == 0

    def exchanged():
        share = own_rows.shape[0] // cores
        block = lax.dynamic_slice_in_dim(own_rows, core * share, share, axis=0)
        parts = []
        for k in range(ring):
            to = z ^ k if swaps else (z + k) % ring
            part = lax.dynamic_slice_in_dim(block, to * depth, depth, axis=1)
            if k:
                pairs = [(i, i ^ k if swaps else (i + k) % ring) for i in range(ring)]
                part = lax.ppermute(part, "feat", pairs)
            parts.append(part)
        every = lax.all_gather(jnp.stack(parts), "tok", axis=1, tiled=True)
        order = [z ^ ((z - k) % ring) if swaps else k for k in range(ring)]
        every = [lax.dynamic_index_in_dim(every, i, axis=0, keepdims=False) for i in order]
        return [
            jnp.concatenate([part[group * rows : (group + 1) * rows] for part in every], axis=0)
            for group in range(GROUPS)
        ]

    columns = exchanged()

    def partial_sums(group, chunk):
        part = jnp.dot(
            columns[group], weight[:, chunk * width : (chunk + 1) * width], preferred_element_type=F32
        ).astype(BF16)
        return [part[k * rows : (k + 1) * rows] for k in range(ring)]

    units = [(group, chunk) for group in range(GROUPS) for chunk in range(CHUNKS)]
    finished = {}
    decoded = {}
    waiting = []
    ordered = [None]
    last = []
    totals = {}
    residuals = {}

    def after(values, others):
        others = [x for x in jax.tree.leaves(others) if x is not None]
        return lax.optimization_barrier((values, others))[0] if others else values

    def background(sent):
        ordered[0] = sent
        for _ in range(min(PIECES, len(waiting))):
            ordered[0] = sent = waiting.pop(0)(sent)

    early = [0, *range(2, ring - 1)]
    late = [1, ring - 1]

    def decode(unit, own, got):
        group, chunk = unit
        codes = {}

        def selected(places, sent):
            used = {slot for m in places if m for slot in (m - 1, ring - m - 1)}
            needed = tuple({slot: came[slot] for slot in sorted(used & set(came))} for came in got)
            mine, (even, other) = after((own, needed), sent)
            zero = jnp.zeros_like(mine)
            parts = []
            for m in places:
                a, b = m - 1, ring - m - 1
                left = jnp.where(odd, even.get(a, zero), other.get(a, zero))
                right = jnp.where(odd, other.get(b, zero), even.get(b, zero))
                parts.append(jnp.where(m <= z, left, right) if m else mine)
            return jnp.concatenate(parts, axis=0)

        def piece(layer, places):
            def run(sent):
                key = tuple(places)
                if key not in codes:
                    codes[key] = selected(places, sent)
                out = lax.dot_general(
                    after(codes[key], sent),
                    decoders[layer, :, chunk * width : (chunk + 1) * width],
                    (((1,), (1,)), ((), ())),
                    preferred_element_type=F32,
                )
                key = group, layer, len(places)
                if places is late:
                    key = group, layer, 0
                decoded[key] = out if key not in decoded else decoded[key] + out
                return decoded[key]

            return run

        if group < GROUPS - 1:
            waiting.extend(piece(layer, early + late) for layer in reversed(range(layers)))
        else:
            last.append(piece)

    def decoded_blocks(group, layer):
        if (group, layer, ring) in decoded:
            return decoded[group, layer, ring]
        return jnp.concatenate([decoded[group, layer, len(early)], decoded[group, layer, 0]], axis=0)

    def place_of(block):
        m = (z - block) % ring
        return jnp.where(m == 1, ring - 2, jnp.where((m == 0) | (m == ring - 1), m, m - 1))

    class Stream:
        def __init__(self, own):
            self.own = own
            self.step = 0
            self.slot = 1
            self.got = [{}, {}]
            self.sums = partial_sums(*own[0])

        def swap(self, value, side):
            i, k, n = self.step, self.slot, len(self.own)
            pairs = []
            for p in range(side, ring - 1, 2):
                q = ring - 2 - p
                if not (i == 0 and p >= k or i == n and p < k):
                    pairs.append((p, p + 1))
                if not (i == 0 and q >= k or i == n and q < k):
                    pairs.append((p + 1, p))
            return lax.ppermute(value, "feat", pairs) if pairs else None

        def advance(self):
            i, k, n = self.step, self.slot, len(self.own)
            sent = []
            for side in range(2):
                if k == 0:
                    sent.append(finished[self.own[i - 1]])
                    continue
                value = self.got[1 - side].get(k - 1)
                if value is not None:
                    value = after(value, ordered)
                if i < n:
                    rightward = odd == (side == 1)
                    zero = jnp.zeros_like(self.sums[k])
                    own = jnp.where(
                        rightward,
                        jnp.where(k > z, self.sums[k], zero),
                        jnp.where(k > ring - 1 - z, self.sums[ring - k], zero),
                    )
                    value = own if value is None else (own.astype(F32) + value.astype(F32)).astype(BF16)
                sent.append(value)
            for side in range(2):
                got = self.swap(sent[side], side) if sent[side] is not None else None
                if got is not None:
                    self.got[side][k] = got
            if i < n or k < ring - 2:
                background(sent)
            self.sent = sent
            if i and k == ring - 2:
                unit = self.own[i - 1]
                decode(unit, finished[unit], tuple(dict(got) for got in self.got))
            self.slot += 1
            if i < n and k == ring - 1:
                chunk = self.own[i][1]
                bias = enc_bias[0, chunk * width : (chunk + 1) * width][None, :]
                total = self.sums[0].astype(F32) + self.got[0][k].astype(F32) + self.got[1][k].astype(F32)
                finished[self.own[i]] = jax.nn.relu(total + bias).astype(BF16)
                self.slot, self.step = 0, i + 1
                if i + 1 < n:
                    self.sums = partial_sums(*self.own[i + 1])
                self.got = [{}, {}]
                return True
            return not (i == n and k == ring - 2)

    def share_cores(group, sent, first=1):
        blocks = after([decoded_blocks(group, layer) for layer in range(first, layers if first else 1)], sent)
        blocks = jnp.stack(blocks).reshape(-1, ring, rows, depth)

        def share(index):
            begin = index * per_core
            return jnp.stack(
                [
                    lax.dynamic_index_in_dim(blocks, place_of(begin + b), axis=1, keepdims=False)
                    for b in range(per_core)
                ],
                axis=1,
            )

        total = share(core)
        given = []
        for k in range(1, cores):
            given.append(share((core + k) % cores).astype(BF16))
            got = lax.ppermute(given[-1], "tok", [(i, (i + k) % cores) for i in range(cores)])
            total += got.astype(F32)
        totals[group, first] = total
        return given

    def share_segments(group, sent):
        total = after(totals[group, 1], sent)
        paired = segments & (segments - 1) == 0
        received, given = [], []
        for k in range(1, segments):
            place = segment ^ k if paired else jnp.minimum(segment + k, layers - 1)
            given.append(lax.dynamic_index_in_dim(total, jnp.maximum(place, 1) - 1, axis=0, keepdims=False).astype(BF16))
            pairs = [(i, i ^ k if paired else i + k) for i in range(segments)]
            got = lax.ppermute(given[-1], "segment", [(i, j) for i, j in pairs if i < j < segments])
            received.append(got)
        own = jnp.where(
            segment == 0,
            totals[group, 0][0],
            lax.dynamic_index_in_dim(total, jnp.maximum(segment, 1) - 1, axis=0, keepdims=False),
        )
        residuals[group] = sum([got.astype(F32) for got in received], own)
        return given

    streams = [Stream(units[i::STREAMS]) for i in range(STREAMS)]
    going = [True] * STREAMS
    while any(going):
        for i, stream in enumerate(streams):
            if going[i]:
                going[i] = stream.advance()
    sent = [stream.sent for stream in streams]
    for work in waiting:
        sent = work(sent)
    for layer in reversed(range(layers)):
        for piece in last:
            sent = piece(layer, early)(sent)
    for group in range(GROUPS - 1):
        sent = share_cores(group, sent)
        share_cores(group, sent, 0)
        sent = share_segments(group, sent)
    for layer in reversed(range(layers)):
        for piece in last:
            sent = piece(layer, late)([sent, residuals.get(GROUPS - 2)] if layer == 0 else sent)
        if layer == 1:
            sent = share_cores(GROUPS - 1, sent)
    share_cores(GROUPS - 1, sent, 0)
    share_segments(GROUPS - 1, sent)
    own = jnp.stack([residuals[group] for group in range(GROUPS)], axis=1)
    residual = targets[0].astype(F32) - own.reshape(targets.shape[1:])
    features = jnp.concatenate(
        [
            jnp.concatenate([finished[group, chunk] for chunk in range(CHUNKS)], axis=1)
            for group in range(GROUPS)
        ],
        axis=0,
    )
    return (features[None], residual[None])


def solution(mesh):
    in_specs = (
        P("segment", "feat", "tok"),
        P("segment", "tok", "feat"),
        P("segment", "feat", "tok"),
        P("segment", "tok"),
        P("segment", None, "feat", "tok"),
    )
    out_specs = (P("segment", "feat", "tok"), P("segment", "tok", "feat"))
    sizes = (mesh.shape["segment"], mesh.shape["feat"], mesh.shape["tok"])
    return jax.shard_map(
        lambda *args: local(*sizes, *args), mesh=mesh, in_specs=in_specs, out_specs=out_specs, check_vma=False
    )
```

```python
import jax
import jax.numpy as jnp
from jax import lax
from jax.sharding import PartitionSpec as P

BF16 = jnp.bfloat16
F32 = jnp.float32
GROUPS = 2
CHUNKS = 2
STREAMS = 2
PIECES = 2


def local(segments, ring, cores, layer_inputs, targets, enc_weight, enc_bias, dec_weight):
    z = lax.axis_index("feat")
    core = lax.axis_index("tok")
    segment = lax.axis_index("segment")
    odd = z % 2 == 1
    rows = layer_inputs.shape[1] // GROUPS
    width = enc_weight.shape[2] // CHUNKS
    depth = enc_weight.shape[1]
    weight = enc_weight[0]
    decoders = dec_weight[0]
    layers = decoders.shape[0]
    per_core = ring // cores

    own_rows = lax.all_gather(layer_inputs[0], "tok", axis=1, tiled=True)

    swaps = ring & (ring - 1) == 0

    def exchanged():
        share = own_rows.shape[0] // cores
        block = lax.dynamic_slice_in_dim(own_rows, core * share, share, axis=0)
        parts = []
        for k in range(ring):
            to = z ^ k if swaps else (z + k) % ring
            part = lax.dynamic_slice_in_dim(block, to * depth, depth, axis=1)
            if k:
                pairs = [(i, i ^ k if swaps else (i + k) % ring) for i in range(ring)]
                part = lax.ppermute(part, "feat", pairs)
            parts.append(part)
        every = lax.all_gather(jnp.stack(parts), "tok", axis=1, tiled=True)
        order = [z ^ ((z - k) % ring) if swaps else k for k in range(ring)]
        every = [lax.dynamic_index_in_dim(every, i, axis=0, keepdims=False) for i in order]
        return [
            jnp.concatenate([part[group * rows : (group + 1) * rows] for part in every], axis=0)
            for group in range(GROUPS)
        ]

    columns = exchanged()

    def partial_sums(group, chunk):
        part = jnp.dot(
            columns[group], weight[:, chunk * width : (chunk + 1) * width], preferred_element_type=F32
        ).astype(BF16)
        return [part[k * rows : (k + 1) * rows] for k in range(ring)]

    units = [(group, chunk) for group in range(GROUPS) for chunk in range(CHUNKS)]
    finished = {}
    decoded = {}
    waiting = []
    ordered = [None]
    last = []
    totals = {}
    residuals = {}

    def after(values, others):
        others = [x for x in jax.tree.leaves(others) if x is not None]
        return lax.optimization_barrier((values, others))[0] if others else values

    def background(sent):
        ordered[0] = sent
        for _ in range(min(PIECES, len(waiting))):
            ordered[0] = sent = waiting.pop(0)(sent)

    every = list(range(ring))

    def decode(unit, own, got):
        group, chunk = unit
        codes = {}

        def selected(places, sent):
            used = {slot for m in places if m for slot in (m - 1, ring - m - 1)}
            needed = tuple({slot: came[slot] for slot in sorted(used & set(came))} for came in got)
            mine, (even, other) = after((own, needed), sent)
            zero = jnp.zeros_like(mine)
            parts = []
            for m in places:
                a, b = m - 1, ring - m - 1
                left = jnp.where(odd, even.get(a, zero), other.get(a, zero))
                right = jnp.where(odd, other.get(b, zero), even.get(b, zero))
                parts.append(jnp.where(m <= z, left, right) if m else mine)
            return jnp.concatenate(parts, axis=0)

        def piece(layer, places):
            def run(sent):
                key = tuple(places)
                if key not in codes:
                    codes[key] = selected(places, sent)
                out = lax.dot_general(
                    after(codes[key], sent),
                    decoders[layer, :, chunk * width : (chunk + 1) * width],
                    (((1,), (1,)), ((), ())),
                    preferred_element_type=F32,
                )
                key = group, layer
                decoded[key] = out if key not in decoded else decoded[key] + out
                return decoded[key]

            return run

        if group < GROUPS - 1:
            waiting.extend(piece(layer, every) for layer in reversed(range(layers)))
        else:
            last.append(piece)

    class Stream:
        def __init__(self, own):
            self.own = own
            self.step = 0
            self.slot = 1
            self.got = [{}, {}]
            self.sums = partial_sums(*own[0])

        def swap(self, value, side):
            i, k, n = self.step, self.slot, len(self.own)
            pairs = []
            for p in range(side, ring - 1, 2):
                q = ring - 2 - p
                if not (i == 0 and p >= k or i == n and p < k):
                    pairs.append((p, p + 1))
                if not (i == 0 and q >= k or i == n and q < k):
                    pairs.append((p + 1, p))
            return lax.ppermute(value, "feat", pairs) if pairs else None

        def advance(self):
            i, k, n = self.step, self.slot, len(self.own)
            sent = []
            for side in range(2):
                if k == 0:
                    sent.append(finished[self.own[i - 1]])
                    continue
                value = self.got[1 - side].get(k - 1)
                if value is not None:
                    value = after(value, ordered)
                if i < n:
                    rightward = odd == (side == 1)
                    zero = jnp.zeros_like(self.sums[k])
                    own = jnp.where(
                        rightward,
                        jnp.where(k > z, self.sums[k], zero),
                        jnp.where(k > ring - 1 - z, self.sums[ring - k], zero),
                    )
                    value = own if value is None else (own.astype(F32) + value.astype(F32)).astype(BF16)
                sent.append(value)
            for side in range(2):
                got = self.swap(sent[side], side) if sent[side] is not None else None
                if got is not None:
                    self.got[side][k] = got
            if i < n or k < ring - 2:
                background(sent)
            self.sent = sent
            if i and k == ring - 2:
                unit = self.own[i - 1]
                decode(unit, finished[unit], tuple(dict(got) for got in self.got))
            self.slot += 1
            if i < n and k == ring - 1:
                chunk = self.own[i][1]
                bias = enc_bias[0, chunk * width : (chunk + 1) * width][None, :]
                total = self.sums[0].astype(F32) + self.got[0][k].astype(F32) + self.got[1][k].astype(F32)
                finished[self.own[i]] = jax.nn.relu(total + bias).astype(BF16)
                self.slot, self.step = 0, i + 1
                if i + 1 < n:
                    self.sums = partial_sums(*self.own[i + 1])
                self.got = [{}, {}]
                return True
            return not (i == n and k == ring - 2)

    def share_cores(group, sent, first=1):
        blocks = after([decoded[group, layer] for layer in range(first, layers if first else 1)], sent)
        blocks = jnp.stack(blocks).reshape(-1, ring, rows, depth)

        def share(index):
            begin = index * per_core
            return jnp.stack(
                [
                    lax.dynamic_index_in_dim(blocks, (z - begin - b) % ring, axis=1, keepdims=False)
                    for b in range(per_core)
                ],
                axis=1,
            )

        total = share(core)
        given = []
        for k in range(1, cores):
            given.append(share((core + k) % cores).astype(BF16))
            got = lax.ppermute(given[-1], "tok", [(i, (i + k) % cores) for i in range(cores)])
            total += got.astype(F32)
        totals[group, first] = total
        return given

    def share_segments(group, sent):
        total = after(totals[group, 1], sent)
        paired = segments & (segments - 1) == 0
        received, given = [], []
        for k in range(1, segments):
            place = segment ^ k if paired else jnp.minimum(segment + k, layers - 1)
            given.append(lax.dynamic_index_in_dim(total, jnp.maximum(place, 1) - 1, axis=0, keepdims=False).astype(BF16))
            pairs = [(i, i ^ k if paired else i + k) for i in range(segments)]
            got = lax.ppermute(given[-1], "segment", [(i, j) for i, j in pairs if i < j < segments])
            received.append(got)
        own = jnp.where(
            segment == 0,
            totals[group, 0][0],
            lax.dynamic_index_in_dim(total, jnp.maximum(segment, 1) - 1, axis=0, keepdims=False),
        )
        residuals[group] = sum([got.astype(F32) for got in received], own)
        return given

    streams = [Stream(units[i::STREAMS]) for i in range(STREAMS)]
    going = [True] * STREAMS
    while any(going):
        for i, stream in enumerate(streams):
            if going[i]:
                going[i] = stream.advance()
    sent = [stream.sent for stream in streams]
    for work in waiting:
        sent = work(sent)
    for group in range(GROUPS - 1):
        sent = share_cores(group, sent)
        share_cores(group, sent, 0)
        sent = share_segments(group, sent)
    for layer in reversed(range(layers)):
        for piece in last:
            sent = piece(layer, every)([sent, residuals.get(GROUPS - 2)] if layer == 0 else sent)
        if layer == 1:
            sent = share_cores(GROUPS - 1, sent)
    share_cores(GROUPS - 1, sent, 0)
    share_segments(GROUPS - 1, sent)
    own = jnp.stack([residuals[group] for group in range(GROUPS)], axis=1)
    residual = targets[0].astype(F32) - own.reshape(targets.shape[1:])
    features = jnp.concatenate(
        [
            jnp.concatenate([finished[group, chunk] for chunk in range(CHUNKS)], axis=1)
            for group in range(GROUPS)
        ],
        axis=0,
    )
    return (features[None], residual[None])


def solution(mesh):
    in_specs = (
        P("segment", "feat", "tok"),
        P("segment", "tok", "feat"),
        P("segment", "feat", "tok"),
        P("segment", "tok"),
        P("segment", None, "feat", "tok"),
    )
    out_specs = (P("segment", "feat", "tok"), P("segment", "tok", "feat"))
    sizes = (mesh.shape["segment"], mesh.shape["feat"], mesh.shape["tok"])
    return jax.shard_map(
        lambda *args: local(*sizes, *args), mesh=mesh, in_specs=in_specs, out_specs=out_specs, check_vma=False
    )
```

```python
import jax
import jax.numpy as jnp
from jax import lax
from jax.sharding import PartitionSpec as P

BF16 = jnp.bfloat16
F32 = jnp.float32
GROUPS = 2
CHUNKS = 2
STREAMS = 2
PIECES = 2


def local(segments, ring, cores, layer_inputs, targets, enc_weight, enc_bias, dec_weight):
    z = lax.axis_index("feat")
    core = lax.axis_index("tok")
    segment = lax.axis_index("segment")
    odd = z % 2 == 1
    rows = layer_inputs.shape[1] // GROUPS
    width = enc_weight.shape[2] // CHUNKS
    depth = enc_weight.shape[1]
    weight = enc_weight[0]
    decoders = dec_weight[0]
    layers = decoders.shape[0]
    per_core = ring // cores

    own_rows = lax.all_gather(layer_inputs[0], "tok", axis=1, tiled=True)

    swaps = ring & (ring - 1) == 0

    def exchanged():
        share = own_rows.shape[0] // cores
        block = lax.dynamic_slice_in_dim(own_rows, core * share, share, axis=0)
        parts = []
        for k in range(ring):
            to = z ^ k if swaps else (z + k) % ring
            part = lax.dynamic_slice_in_dim(block, to * depth, depth, axis=1)
            if k:
                pairs = [(i, i ^ k if swaps else (i + k) % ring) for i in range(ring)]
                part = lax.ppermute(part, "feat", pairs)
            parts.append(part)
        every = lax.all_gather(jnp.stack(parts), "tok", axis=1, tiled=True)
        order = [z ^ ((z - k) % ring) if swaps else k for k in range(ring)]
        every = [lax.dynamic_index_in_dim(every, i, axis=0, keepdims=False) for i in order]
        return [
            jnp.concatenate([part[group * rows : (group + 1) * rows] for part in every], axis=0)
            for group in range(GROUPS)
        ]

    columns = exchanged()

    def partial_sums(group, chunk, sent=None):
        part = jnp.dot(
            after(columns[group], sent), weight[:, chunk * width : (chunk + 1) * width], preferred_element_type=F32
        ).astype(BF16)
        return [part[k * rows : (k + 1) * rows] for k in range(ring)]

    units = [(group, chunk) for group in range(GROUPS) for chunk in range(CHUNKS)]
    finished = {}
    decoded = {}
    waiting = []
    ordered = [None]
    last = []
    totals = {}
    residuals = {}

    def after(values, others):
        others = [x for x in jax.tree.leaves(others) if x is not None]
        return lax.optimization_barrier((values, others))[0] if others else values

    def background(sent):
        ordered[0] = sent
        for _ in range(min(PIECES, len(waiting))):
            ordered[0] = sent = waiting.pop(0)(sent)

    every = list(range(ring))

    def decode(unit, own, got):
        group, chunk = unit
        codes = {}

        def selected(places, sent):
            used = {slot for m in places if m for slot in (m - 1, ring - m - 1)}
            needed = tuple({slot: came[slot] for slot in sorted(used & set(came))} for came in got)
            mine, (even, other) = after((own, needed), sent)
            zero = jnp.zeros_like(mine)
            parts = []
            for m in places:
                a, b = m - 1, ring - m - 1
                left = jnp.where(odd, even.get(a, zero), other.get(a, zero))
                right = jnp.where(odd, other.get(b, zero), even.get(b, zero))
                parts.append(jnp.where(m <= z, left, right) if m else mine)
            return jnp.concatenate(parts, axis=0)

        def piece(layer, places):
            def run(sent):
                key = tuple(places)
                if key not in codes:
                    codes[key] = selected(places, sent)
                out = lax.dot_general(
                    after(codes[key], sent),
                    decoders[layer, :, chunk * width : (chunk + 1) * width],
                    (((1,), (1,)), ((), ())),
                    preferred_element_type=F32,
                )
                key = group, layer
                decoded[key] = out if key not in decoded else decoded[key] + out
                return decoded[key]

            return run

        if group < GROUPS - 1:
            waiting.extend(piece(layer, every) for layer in reversed(range(layers)))
        else:
            last.append(piece)

    class Stream:
        def __init__(self, own):
            self.own = own
            self.step = 0
            self.slot = 1
            self.got = [{}, {}]
            self.sums = None

        def swap(self, value, side):
            i, k, n = self.step, self.slot, len(self.own)
            pairs = []
            for p in range(side, ring - 1, 2):
                q = ring - 2 - p
                if not (i == 0 and p >= k or i == n and p < k):
                    pairs.append((p, p + 1))
                if not (i == 0 and q >= k or i == n and q < k):
                    pairs.append((p + 1, p))
            return lax.ppermute(value, "feat", pairs) if pairs else None

        def advance(self):
            i, k, n = self.step, self.slot, len(self.own)
            if self.sums is None:
                self.sums = partial_sums(*self.own[0], ordered)
            sent = []
            for side in range(2):
                if k == 0:
                    sent.append(finished[self.own[i - 1]])
                    continue
                value = self.got[1 - side].get(k - 1)
                if value is not None:
                    value = after(value, ordered)
                if i < n:
                    rightward = odd == (side == 1)
                    zero = jnp.zeros_like(self.sums[k])
                    own = jnp.where(
                        rightward,
                        jnp.where(k > z, self.sums[k], zero),
                        jnp.where(k > ring - 1 - z, self.sums[ring - k], zero),
                    )
                    value = own if value is None else (own.astype(F32) + value.astype(F32)).astype(BF16)
                sent.append(value)
            for side in range(2):
                got = self.swap(sent[side], side) if sent[side] is not None else None
                if got is not None:
                    self.got[side][k] = got
            if i < n or k < ring - 2:
                background(sent)
            self.sent = sent
            if i and k == ring - 2:
                unit = self.own[i - 1]
                decode(unit, finished[unit], tuple(dict(got) for got in self.got))
            self.slot += 1
            if i < n and k == ring - 1:
                chunk = self.own[i][1]
                bias = enc_bias[0, chunk * width : (chunk + 1) * width][None, :]
                total = self.sums[0].astype(F32) + self.got[0][k].astype(F32) + self.got[1][k].astype(F32)
                finished[self.own[i]] = jax.nn.relu(total + bias).astype(BF16)
                self.slot, self.step = 0, i + 1
                if i + 1 < n:
                    self.sums = partial_sums(*self.own[i + 1])
                self.got = [{}, {}]
                return True
            return not (i == n and k == ring - 2)

    def share_cores(group, sent, first=1):
        blocks = after([decoded[group, layer] for layer in range(first, layers if first else 1)], sent)
        blocks = jnp.stack(blocks).reshape(-1, ring, rows, depth)

        def share(index):
            begin = index * per_core
            return jnp.stack(
                [
                    lax.dynamic_index_in_dim(blocks, (z - begin - b) % ring, axis=1, keepdims=False)
                    for b in range(per_core)
                ],
                axis=1,
            )

        total = share(core)
        given = []
        for k in range(1, cores):
            given.append(share((core + k) % cores).astype(BF16))
            got = lax.ppermute(given[-1], "tok", [(i, (i + k) % cores) for i in range(cores)])
            total += got.astype(F32)
        totals[group, first] = total
        return given

    def share_segments(group, sent):
        total = after(totals[group, 1], sent)
        paired = segments & (segments - 1) == 0
        received, given = [], []
        for k in range(1, segments):
            place = segment ^ k if paired else jnp.minimum(segment + k, layers - 1)
            given.append(lax.dynamic_index_in_dim(total, jnp.maximum(place, 1) - 1, axis=0, keepdims=False).astype(BF16))
            pairs = [(i, i ^ k if paired else i + k) for i in range(segments)]
            got = lax.ppermute(given[-1], "segment", [(i, j) for i, j in pairs if i < j < segments])
            received.append(got)
        own = jnp.where(
            segment == 0,
            totals[group, 0][0],
            lax.dynamic_index_in_dim(total, jnp.maximum(segment, 1) - 1, axis=0, keepdims=False),
        )
        residuals[group] = sum([got.astype(F32) for got in received], own)
        return given

    streams = [Stream(units[i::STREAMS]) for i in range(STREAMS)]
    going = [True] * STREAMS
    while any(going):
        for i, stream in enumerate(streams):
            if going[i]:
                going[i] = stream.advance()
    sent = [stream.sent for stream in streams]
    for work in waiting:
        sent = work(sent)
    for group in range(GROUPS - 1):
        sent = share_cores(group, sent)
        share_cores(group, sent, 0)
        sent = share_segments(group, sent)
    for layer in reversed(range(layers)):
        for piece in last:
            sent = piece(layer, every)([sent, residuals.get(GROUPS - 2)] if layer == 0 else sent)
        if layer == 1:
            sent = share_cores(GROUPS - 1, sent)
    share_cores(GROUPS - 1, sent, 0)
    share_segments(GROUPS - 1, sent)
    own = jnp.stack([residuals[group] for group in range(GROUPS)], axis=1)
    residual = targets[0].astype(F32) - own.reshape(targets.shape[1:])
    features = jnp.concatenate(
        [
            jnp.concatenate([finished[group, chunk] for chunk in range(CHUNKS)], axis=1)
            for group in range(GROUPS)
        ],
        axis=0,
    )
    return (features[None], residual[None])


def solution(mesh):
    in_specs = (
        P("segment", "feat", "tok"),
        P("segment", "tok", "feat"),
        P("segment", "feat", "tok"),
        P("segment", "tok"),
        P("segment", None, "feat", "tok"),
    )
    out_specs = (P("segment", "feat", "tok"), P("segment", "tok", "feat"))
    sizes = (mesh.shape["segment"], mesh.shape["feat"], mesh.shape["tok"])
    return jax.shard_map(
        lambda *args: local(*sizes, *args), mesh=mesh, in_specs=in_specs, out_specs=out_specs, check_vma=False
    )
```

```python
import jax
import jax.numpy as jnp
from jax import lax
from jax.sharding import PartitionSpec as P

BF16 = jnp.bfloat16
F32 = jnp.float32
GROUPS = 2
CHUNKS = 2
STREAMS = 2
PIECES = 2


def local(segments, ring, cores, layer_inputs, targets, enc_weight, enc_bias, dec_weight):
    z = lax.axis_index("feat")
    core = lax.axis_index("tok")
    segment = lax.axis_index("segment")
    odd = z % 2 == 1
    rows = layer_inputs.shape[1] // GROUPS
    width = enc_weight.shape[2] // CHUNKS
    depth = enc_weight.shape[1]
    weight = enc_weight[0]
    decoders = dec_weight[0]
    layers = decoders.shape[0]
    per_core = ring // cores

    own_rows = lax.all_gather(layer_inputs[0], "tok", axis=1, tiled=True)

    swaps = ring & (ring - 1) == 0

    def exchanged():
        share = own_rows.shape[0] // cores
        block = lax.dynamic_slice_in_dim(own_rows, core * share, share, axis=0)
        parts = []
        for k in range(ring):
            to = z ^ k if swaps else (z + k) % ring
            part = lax.dynamic_slice_in_dim(block, to * depth, depth, axis=1)
            if k:
                pairs = [(i, i ^ k if swaps else (i + k) % ring) for i in range(ring)]
                part = lax.ppermute(part, "feat", pairs)
            parts.append(part)
        every = lax.all_gather(jnp.stack(parts), "tok", axis=1, tiled=True)
        order = [z ^ ((z - k) % ring) if swaps else k for k in range(ring)]
        every = [lax.dynamic_index_in_dim(every, i, axis=0, keepdims=False) for i in order]
        return [
            jnp.concatenate([part[group * rows : (group + 1) * rows] for part in every], axis=0)
            for group in range(GROUPS)
        ]

    columns = exchanged()

    def partial_sums(group, chunk, sent=None):
        part = jnp.dot(
            after(columns[group], sent), weight[:, chunk * width : (chunk + 1) * width], preferred_element_type=F32
        ).astype(BF16)
        return [part[k * rows : (k + 1) * rows] for k in range(ring)]

    units = [(group, chunk) for group in range(GROUPS) for chunk in range(CHUNKS)]
    finished = {}
    decoded = {}
    waiting = []
    ordered = [None]
    last = []
    totals = {}
    residuals = {}
    arrived = {}

    def after(values, others):
        others = [x for x in jax.tree.leaves(others) if x is not None]
        return lax.optimization_barrier((values, others))[0] if others else values

    def background(sent):
        ordered[0] = sent
        for _ in range(min(PIECES, len(waiting))):
            ordered[0] = sent = waiting.pop(0)(sent)

    every = list(range(ring))

    def decode(unit, own, got):
        group, chunk = unit
        codes = {}

        def selected(places, sent):
            used = {slot for m in places if m for slot in (m - 1, ring - m - 1)}
            needed = tuple({slot: came[slot] for slot in sorted(used & set(came))} for came in got)
            mine, (even, other) = after((own, needed), sent)
            zero = jnp.zeros_like(mine)
            parts = []
            for m in places:
                a, b = m - 1, ring - m - 1
                left = jnp.where(odd, even.get(a, zero), other.get(a, zero))
                right = jnp.where(odd, other.get(b, zero), even.get(b, zero))
                parts.append(jnp.where(m <= z, left, right) if m else mine)
            return jnp.concatenate(parts, axis=0)

        def piece(layer, places):
            def run(sent):
                key = tuple(places)
                if key not in codes:
                    codes[key] = selected(places, sent)
                out = lax.dot_general(
                    after(codes[key], sent),
                    decoders[layer, :, chunk * width : (chunk + 1) * width],
                    (((1,), (1,)), ((), ())),
                    preferred_element_type=F32,
                )
                key = group, layer
                decoded[key] = out if key not in decoded else decoded[key] + out
                return decoded[key]

            return run

        if group < GROUPS - 1:
            waiting.extend(piece(layer, every) for layer in reversed(range(layers)))
        else:
            last.append(piece)

    class Stream:
        def __init__(self, own):
            self.own = own
            self.step = 0
            self.slot = 1
            self.got = [{}, {}]
            self.sums = None

        def swap(self, value, side):
            i, k, n = self.step, self.slot, len(self.own)
            pairs = []
            for p in range(side, ring - 1, 2):
                q = ring - 2 - p
                if not (i == 0 and p >= k or i == n and p < k):
                    pairs.append((p, p + 1))
                if not (i == 0 and q >= k or i == n and q < k):
                    pairs.append((p + 1, p))
            return lax.ppermute(value, "feat", pairs) if pairs else None

        def advance(self):
            i, k, n = self.step, self.slot, len(self.own)
            if self.sums is None:
                self.sums = partial_sums(*self.own[0], ordered)
            sent = []
            for side in range(2):
                if k == 0:
                    sent.append(finished[self.own[i - 1]])
                    continue
                value = self.got[1 - side].get(k - 1)
                if value is not None:
                    value = after(value, ordered)
                if i < n:
                    rightward = odd == (side == 1)
                    zero = jnp.zeros_like(self.sums[k])
                    own = jnp.where(
                        rightward,
                        jnp.where(k > z, self.sums[k], zero),
                        jnp.where(k > ring - 1 - z, self.sums[ring - k], zero),
                    )
                    value = own if value is None else (own.astype(F32) + value.astype(F32)).astype(BF16)
                sent.append(value)
            for side in range(2):
                got = self.swap(sent[side], side) if sent[side] is not None else None
                if got is not None:
                    self.got[side][k] = got
            if i < n or k < ring - 2:
                background(sent)
            self.sent = sent
            if i and k == ring - 2:
                unit = self.own[i - 1]
                decode(unit, finished[unit], tuple(dict(got) for got in self.got))
            self.slot += 1
            if i < n and k == ring - 1:
                chunk = self.own[i][1]
                bias = enc_bias[0, chunk * width : (chunk + 1) * width][None, :]
                total = self.sums[0].astype(F32) + self.got[0][k].astype(F32) + self.got[1][k].astype(F32)
                finished[self.own[i]] = jax.nn.relu(total + bias).astype(BF16)
                self.slot, self.step = 0, i + 1
                if i + 1 < n:
                    self.sums = partial_sums(*self.own[i + 1])
                self.got = [{}, {}]
                return True
            return not (i == n and k == ring - 2)

    def share_cores(group, sent, first=1):
        blocks = after([decoded[group, layer] for layer in range(first, layers if first else 1)], sent)
        blocks = jnp.stack(blocks).reshape(-1, ring, rows, depth)

        def share(index):
            begin = index * per_core
            return jnp.stack(
                [
                    lax.dynamic_index_in_dim(blocks, (z - begin - b) % ring, axis=1, keepdims=False)
                    for b in range(per_core)
                ],
                axis=1,
            )

        total = share(core)
        given = []
        for k in range(1, cores):
            given.append(share((core + k) % cores).astype(BF16))
            got = lax.ppermute(given[-1], "tok", [(i, (i + k) % cores) for i in range(cores)])
            total += got.astype(F32)
        totals[group, first] = total
        return given

    def share_segments(group, sent):
        total = after(totals[group, 1], sent)
        paired = segments & (segments - 1) == 0
        received, given = [], []
        for k in range(1, segments):
            place = segment ^ k if paired else jnp.minimum(segment + k, layers - 1)
            given.append(lax.dynamic_index_in_dim(total, jnp.maximum(place, 1) - 1, axis=0, keepdims=False).astype(BF16))
            pairs = [(i, i ^ k if paired else i + k) for i in range(segments)]
            got = lax.ppermute(given[-1], "segment", [(i, j) for i, j in pairs if i < j < segments])
            received.append(got)
        arrived[group] = total, received
        return given

    def finish(group):
        total, received = arrived[group]
        own = jnp.where(
            segment == 0,
            totals[group, 0][0],
            lax.dynamic_index_in_dim(total, jnp.maximum(segment, 1) - 1, axis=0, keepdims=False),
        )
        residuals[group] = sum([got.astype(F32) for got in received], own)

    streams = [Stream(units[i::STREAMS]) for i in range(STREAMS)]
    going = [True] * STREAMS
    while any(going):
        for i, stream in enumerate(streams):
            if going[i]:
                going[i] = stream.advance()
    sent = [stream.sent for stream in streams]
    for work in waiting:
        sent = work(sent)
    for group in range(GROUPS - 1):
        sent = share_cores(group, sent)
        share_cores(group, sent, 0)
        sent = share_segments(group, sent)
        finish(group)
    for layer in reversed(range(1, layers)):
        for piece in last:
            sent = piece(layer, every)(sent)
    sent = share_cores(GROUPS - 1, sent)
    sent = share_segments(GROUPS - 1, sent)
    for piece in last:
        sent = piece(0, every)([sent, residuals.get(GROUPS - 2)])
    share_cores(GROUPS - 1, sent, 0)
    finish(GROUPS - 1)
    own = jnp.stack([residuals[group] for group in range(GROUPS)], axis=1)
    residual = targets[0].astype(F32) - own.reshape(targets.shape[1:])
    features = jnp.concatenate(
        [
            jnp.concatenate([finished[group, chunk] for chunk in range(CHUNKS)], axis=1)
            for group in range(GROUPS)
        ],
        axis=0,
    )
    return (features[None], residual[None])


def solution(mesh):
    in_specs = (
        P("segment", "feat", "tok"),
        P("segment", "tok", "feat"),
        P("segment", "feat", "tok"),
        P("segment", "tok"),
        P("segment", None, "feat", "tok"),
    )
    out_specs = (P("segment", "feat", "tok"), P("segment", "tok", "feat"))
    sizes = (mesh.shape["segment"], mesh.shape["feat"], mesh.shape["tok"])
    return jax.shard_map(
        lambda *args: local(*sizes, *args), mesh=mesh, in_specs=in_specs, out_specs=out_specs, check_vma=False
    )
```

```python
import jax
import jax.numpy as jnp
from jax import lax
from jax.sharding import PartitionSpec as P

BF16 = jnp.bfloat16
F32 = jnp.float32
GROUPS = 2
CHUNKS = 2
STREAMS = 2
PIECES = 2


def local(segments, ring, cores, layer_inputs, targets, enc_weight, enc_bias, dec_weight):
    z = lax.axis_index("feat")
    core = lax.axis_index("tok")
    segment = lax.axis_index("segment")
    odd = z % 2 == 1
    rows = layer_inputs.shape[1] // GROUPS
    width = enc_weight.shape[2] // CHUNKS
    depth = enc_weight.shape[1]
    weight = enc_weight[0]
    decoders = dec_weight[0]
    layers = decoders.shape[0]
    per_core = ring // cores

    own_rows = lax.all_gather(layer_inputs[0], "tok", axis=1, tiled=True)

    swaps = ring & (ring - 1) == 0

    def exchanged():
        share = own_rows.shape[0] // cores
        block = lax.dynamic_slice_in_dim(own_rows, core * share, share, axis=0)
        parts = []
        for k in range(ring):
            to = z ^ k if swaps else (z + k) % ring
            part = lax.dynamic_slice_in_dim(block, to * depth, depth, axis=1)
            if k:
                pairs = [(i, i ^ k if swaps else (i + k) % ring) for i in range(ring)]
                part = lax.ppermute(part, "feat", pairs)
            parts.append(part)
        every = lax.all_gather(jnp.stack(parts), "tok", axis=1, tiled=True)
        order = [z ^ ((z - k) % ring) if swaps else k for k in range(ring)]
        every = [lax.dynamic_index_in_dim(every, i, axis=0, keepdims=False) for i in order]
        return [
            jnp.concatenate([part[group * rows : (group + 1) * rows] for part in every], axis=0)
            for group in range(GROUPS)
        ]

    columns = exchanged()

    def partial_sums(group, chunk, sent=None):
        part = jnp.dot(
            after(columns[group], sent), weight[:, chunk * width : (chunk + 1) * width], preferred_element_type=F32
        ).astype(BF16)
        return [part[k * rows : (k + 1) * rows] for k in range(ring)]

    units = [(group, chunk) for group in range(GROUPS) for chunk in range(CHUNKS)]
    finished = {}
    decoded = {}
    waiting = []
    ordered = [None]
    last = []
    totals = {}
    residuals = {}
    arrived = {}

    def after(values, others):
        others = [x for x in jax.tree.leaves(others) if x is not None]
        return lax.optimization_barrier((values, others))[0] if others else values

    def background(sent):
        ordered[0] = sent
        for _ in range(min(PIECES, len(waiting))):
            ordered[0] = sent = waiting.pop(0)(sent)

    every = list(range(ring))

    def decode(unit, own, got):
        group, chunk = unit
        codes = {}

        def selected(places, sent):
            used = {slot for m in places if m for slot in (m - 1, ring - m - 1)}
            needed = tuple({slot: came[slot] for slot in sorted(used & set(came))} for came in got)
            mine, (even, other) = after((own, needed), sent)
            zero = jnp.zeros_like(mine)
            parts = []
            for m in places:
                a, b = m - 1, ring - m - 1
                left = jnp.where(odd, even.get(a, zero), other.get(a, zero))
                right = jnp.where(odd, other.get(b, zero), even.get(b, zero))
                parts.append(jnp.where(m <= z, left, right) if m else mine)
            return jnp.concatenate(parts, axis=0)

        def piece(layer, places):
            def run(sent):
                key = tuple(places)
                if key not in codes:
                    codes[key] = selected(places, sent)
                out = lax.dot_general(
                    after(codes[key], sent),
                    decoders[layer, :, chunk * width : (chunk + 1) * width],
                    (((1,), (1,)), ((), ())),
                    preferred_element_type=F32,
                )
                key = group, layer
                decoded[key] = out if key not in decoded else decoded[key] + out
                return decoded[key]

            return run

        if group < GROUPS - 1:
            waiting.extend(piece(layer, every) for layer in reversed(range(layers)))
        else:
            last.append(piece)

    class Stream:
        def __init__(self, own):
            self.own = own
            self.step = 0
            self.slot = 1
            self.got = [{}, {}]
            self.sums = None

        def swap(self, value, side):
            i, k, n = self.step, self.slot, len(self.own)
            pairs = []
            for p in range(side, ring - 1, 2):
                q = ring - 2 - p
                if not (i == 0 and p >= k or i == n and p < k):
                    pairs.append((p, p + 1))
                if not (i == 0 and q >= k or i == n and q < k):
                    pairs.append((p + 1, p))
            return lax.ppermute(value, "feat", pairs) if pairs else None

        def advance(self):
            i, k, n = self.step, self.slot, len(self.own)
            if self.sums is None:
                self.sums = partial_sums(*self.own[0], ordered)
            sent = []
            for side in range(2):
                if k == 0:
                    sent.append(finished[self.own[i - 1]])
                    continue
                value = self.got[1 - side].get(k - 1)
                if value is not None:
                    value = after(value, ordered)
                if i < n:
                    rightward = odd == (side == 1)
                    zero = jnp.zeros_like(self.sums[k])
                    own = jnp.where(
                        rightward,
                        jnp.where(k > z, self.sums[k], zero),
                        jnp.where(k > ring - 1 - z, self.sums[ring - k], zero),
                    )
                    value = own if value is None else (own.astype(F32) + value.astype(F32)).astype(BF16)
                sent.append(value)
            for side in range(2):
                got = self.swap(sent[side], side) if sent[side] is not None else None
                if got is not None:
                    self.got[side][k] = got
            if i < n or k < ring - 2:
                background(sent)
            self.sent = sent
            if i and k == ring - 2:
                unit = self.own[i - 1]
                decode(unit, finished[unit], tuple(dict(got) for got in self.got))
            self.slot += 1
            if i < n and k == ring - 1:
                chunk = self.own[i][1]
                bias = enc_bias[0, chunk * width : (chunk + 1) * width][None, :]
                total = self.sums[0].astype(F32) + self.got[0][k].astype(F32) + self.got[1][k].astype(F32)
                finished[self.own[i]] = jax.nn.relu(total + bias).astype(BF16)
                self.slot, self.step = 0, i + 1
                if i + 1 < n:
                    self.sums = partial_sums(*self.own[i + 1])
                self.got = [{}, {}]
                return True
            return not (i == n and k == ring - 2)

    def share_cores(group, sent, first=1):
        blocks = after([decoded[group, layer] for layer in range(first, layers if first else 1)], sent)
        blocks = jnp.stack(blocks).reshape(-1, ring, rows, depth)

        def share(index):
            begin = index * per_core
            return jnp.stack(
                [
                    lax.dynamic_index_in_dim(blocks, (z - begin - b) % ring, axis=1, keepdims=False)
                    for b in range(per_core)
                ],
                axis=1,
            )

        total = share(core)
        given = []
        for k in range(1, cores):
            given.append(share((core + k) % cores).astype(BF16))
            got = lax.ppermute(given[-1], "tok", [(i, (i + k) % cores) for i in range(cores)])
            total += got.astype(F32)
        totals[group, first] = total
        return given

    def share_segments(group, sent):
        total = after(totals[group, 1], sent)
        paired = segments & (segments - 1) == 0
        received, given = [], []
        for k in range(1, segments):
            place = segment ^ k if paired else jnp.minimum(segment + k, layers - 1)
            given.append(lax.dynamic_index_in_dim(total, jnp.maximum(place, 1) - 1, axis=0, keepdims=False).astype(BF16))
            pairs = [(i, i ^ k if paired else i + k) for i in range(segments)]
            got = lax.ppermute(given[-1], "segment", [(i, j) for i, j in pairs if i < j < segments])
            received.append(got)
        arrived[group] = total, received
        return given

    def finish(group):
        total, received = arrived[group]
        own = jnp.where(
            segment == 0,
            totals[group, 0][0],
            lax.dynamic_index_in_dim(total, jnp.maximum(segment, 1) - 1, axis=0, keepdims=False),
        )
        residuals[group] = sum([got.astype(F32) for got in received], own)

    streams = [Stream(units[i::STREAMS]) for i in range(STREAMS)]
    going = [True] * STREAMS
    while any(going):
        for i, stream in enumerate(streams):
            if going[i]:
                going[i] = stream.advance()
    sent = [stream.sent for stream in streams]
    for work in waiting:
        sent = work(sent)
    for group in range(GROUPS - 1):
        sent = share_cores(group, sent)
        share_cores(group, sent, 0)
        sent = share_segments(group, sent)
        finish(group)
    for layer in reversed(range(1, layers)):
        for piece in last:
            sent = piece(layer, every)([sent, residuals.get(GROUPS - 2)] if layer == 1 else sent)
    sent = share_cores(GROUPS - 1, sent)
    sent = share_segments(GROUPS - 1, sent)
    for piece in last:
        sent = piece(0, every)(sent)
    share_cores(GROUPS - 1, sent, 0)
    finish(GROUPS - 1)
    own = jnp.stack([residuals[group] for group in range(GROUPS)], axis=1)
    residual = targets[0].astype(F32) - own.reshape(targets.shape[1:])
    features = jnp.concatenate(
        [
            jnp.concatenate([finished[group, chunk] for chunk in range(CHUNKS)], axis=1)
            for group in range(GROUPS)
        ],
        axis=0,
    )
    return (features[None], residual[None])


def solution(mesh):
    in_specs = (
        P("segment", "feat", "tok"),
        P("segment", "tok", "feat"),
        P("segment", "feat", "tok"),
        P("segment", "tok"),
        P("segment", None, "feat", "tok"),
    )
    out_specs = (P("segment", "feat", "tok"), P("segment", "tok", "feat"))
    sizes = (mesh.shape["segment"], mesh.shape["feat"], mesh.shape["tok"])
    return jax.shard_map(
        lambda *args: local(*sizes, *args), mesh=mesh, in_specs=in_specs, out_specs=out_specs, check_vma=False
    )
```

```python
import jax
import jax.numpy as jnp
from jax import lax
from jax.sharding import PartitionSpec as P

BF16 = jnp.bfloat16
F32 = jnp.float32
GROUPS = 2
CHUNKS = 2
STREAMS = 2
PIECES = 2


def local(segments, ring, cores, layer_inputs, targets, enc_weight, enc_bias, dec_weight):
    z = lax.axis_index("feat")
    core = lax.axis_index("tok")
    segment = lax.axis_index("segment")
    odd = z % 2 == 1
    rows = layer_inputs.shape[1] // GROUPS
    width = enc_weight.shape[2] // CHUNKS
    depth = enc_weight.shape[1]
    weight = enc_weight[0]
    decoders = dec_weight[0]
    layers = decoders.shape[0]
    per_core = ring // cores

    own_rows = lax.all_gather(layer_inputs[0], "tok", axis=1, tiled=True)

    swaps = ring & (ring - 1) == 0

    def exchanged():
        share = own_rows.shape[0] // cores
        block = lax.dynamic_slice_in_dim(own_rows, core * share, share, axis=0)
        parts = []
        for k in range(ring):
            to = z ^ k if swaps else (z + k) % ring
            part = lax.dynamic_slice_in_dim(block, to * depth, depth, axis=1)
            if k:
                pairs = [(i, i ^ k if swaps else (i + k) % ring) for i in range(ring)]
                part = lax.ppermute(part, "feat", pairs)
            parts.append(part)
        every = lax.all_gather(jnp.stack(parts), "tok", axis=1, tiled=True)
        order = [z ^ ((z - k) % ring) if swaps else k for k in range(ring)]
        every = [lax.dynamic_index_in_dim(every, i, axis=0, keepdims=False) for i in order]
        return [
            jnp.concatenate([part[group * rows : (group + 1) * rows] for part in every], axis=0)
            for group in range(GROUPS)
        ]

    columns = exchanged()

    def partial_sums(group, chunk, sent=None):
        part = jnp.dot(
            after(columns[group], sent), weight[:, chunk * width : (chunk + 1) * width], preferred_element_type=F32
        ).astype(BF16)
        return [part[k * rows : (k + 1) * rows] for k in range(ring)]

    units = [(group, chunk) for group in range(GROUPS) for chunk in range(CHUNKS)]
    finished = {}
    decoded = {}
    waiting = []
    ordered = [None]
    last = []
    totals = {}
    residuals = {}
    arrived = {}

    def after(values, others):
        others = [x for x in jax.tree.leaves(others) if x is not None]
        return lax.optimization_barrier((values, others))[0] if others else values

    def background(sent):
        ordered[0] = sent
        for _ in range(min(PIECES, len(waiting))):
            ordered[0] = sent = waiting.pop(0)(sent)

    every = list(range(ring))

    def decode(unit, own, got):
        group, chunk = unit
        codes = {}

        def selected(places, sent):
            used = {slot for m in places if m for slot in (m - 1, ring - m - 1)}
            needed = tuple({slot: came[slot] for slot in sorted(used & set(came))} for came in got)
            mine, (even, other) = after((own, needed), sent)
            zero = jnp.zeros_like(mine)
            parts = []
            for m in places:
                a, b = m - 1, ring - m - 1
                left = jnp.where(odd, even.get(a, zero), other.get(a, zero))
                right = jnp.where(odd, other.get(b, zero), even.get(b, zero))
                parts.append(jnp.where(m <= z, left, right) if m else mine)
            return jnp.concatenate(parts, axis=0)

        def piece(layer, places):
            def run(sent):
                key = tuple(places)
                if key not in codes:
                    codes[key] = selected(places, sent)
                out = lax.dot_general(
                    after(codes[key], sent),
                    decoders[layer, :, chunk * width : (chunk + 1) * width],
                    (((1,), (1,)), ((), ())),
                    preferred_element_type=F32,
                )
                key = group, layer
                decoded[key] = out if key not in decoded else decoded[key] + out
                return decoded[key]

            return run

        if group < GROUPS - 1:
            waiting.extend(piece(layer, every) for layer in reversed(range(layers)))
        else:
            last.append(piece)

    class Stream:
        def __init__(self, own):
            self.own = own
            self.step = 0
            self.slot = 1
            self.got = [{}, {}]
            self.sums = None

        def swap(self, value, side):
            i, k, n = self.step, self.slot, len(self.own)
            pairs = []
            for p in range(side, ring - 1, 2):
                q = ring - 2 - p
                if not (i == 0 and p >= k or i == n and p < k):
                    pairs.append((p, p + 1))
                if not (i == 0 and q >= k or i == n and q < k):
                    pairs.append((p + 1, p))
            return lax.ppermute(value, "feat", pairs) if pairs else None

        def advance(self):
            i, k, n = self.step, self.slot, len(self.own)
            if self.sums is None:
                self.sums = partial_sums(*self.own[0], ordered)
            sent = []
            for side in range(2):
                if k == 0:
                    sent.append(finished[self.own[i - 1]])
                    continue
                value = self.got[1 - side].get(k - 1)
                if value is not None:
                    value = after(value, ordered)
                if i < n:
                    rightward = odd == (side == 1)
                    zero = jnp.zeros_like(self.sums[k])
                    own = jnp.where(
                        rightward,
                        jnp.where(k > z, self.sums[k], zero),
                        jnp.where(k > ring - 1 - z, self.sums[ring - k], zero),
                    )
                    value = own if value is None else (own.astype(F32) + value.astype(F32)).astype(BF16)
                sent.append(value)
            for side in range(2):
                got = self.swap(sent[side], side) if sent[side] is not None else None
                if got is not None:
                    self.got[side][k] = got
            if i < n or k < ring - 2:
                background(sent)
            self.sent = sent
            if i and k == ring - 2:
                unit = self.own[i - 1]
                decode(unit, finished[unit], tuple(dict(got) for got in self.got))
            self.slot += 1
            if i < n and k == ring - 1:
                chunk = self.own[i][1]
                bias = enc_bias[0, chunk * width : (chunk + 1) * width][None, :]
                total = self.sums[0].astype(F32) + self.got[0][k].astype(F32) + self.got[1][k].astype(F32)
                finished[self.own[i]] = jax.nn.relu(total + bias).astype(BF16)
                self.slot, self.step = 0, i + 1
                if i + 1 < n:
                    self.sums = partial_sums(*self.own[i + 1])
                self.got = [{}, {}]
                return True
            return not (i == n and k == ring - 2)

    def share_cores(group, sent, first=1):
        blocks = after([decoded[group, layer] for layer in range(first, layers if first else 1)], sent)
        blocks = jnp.stack(blocks).reshape(-1, ring, rows, depth)

        def share(index):
            begin = index * per_core
            return jnp.stack(
                [
                    lax.dynamic_index_in_dim(blocks, (z - begin - b) % ring, axis=1, keepdims=False)
                    for b in range(per_core)
                ],
                axis=1,
            )

        total = share(core)
        given = []
        for k in range(1, cores):
            given.append(share((core + k) % cores).astype(BF16))
            got = lax.ppermute(given[-1], "tok", [(i, (i + k) % cores) for i in range(cores)])
            total += got.astype(F32)
        totals[group, first] = total
        return given

    def share_segments(group, sent):
        total = after(totals[group, 1], sent)
        paired = segments & (segments - 1) == 0
        received, given = [], []
        for k in range(1, segments):
            place = segment ^ k if paired else jnp.minimum(segment + k, layers - 1)
            given.append(lax.dynamic_index_in_dim(total, jnp.maximum(place, 1) - 1, axis=0, keepdims=False).astype(BF16))
            pairs = [(i, i ^ k if paired else i + k) for i in range(segments)]
            got = lax.ppermute(given[-1], "segment", [(i, j) for i, j in pairs if i < j < segments])
            received.append(got)
        arrived[group] = total, received
        return given

    def finish(group):
        total, received = arrived[group]
        own = jnp.where(
            segment == 0,
            totals[group, 0][0],
            lax.dynamic_index_in_dim(total, jnp.maximum(segment, 1) - 1, axis=0, keepdims=False),
        )
        residuals[group] = sum([got.astype(F32) for got in received], own)

    streams = [Stream(units[i::STREAMS]) for i in range(STREAMS)]
    going = [True] * STREAMS
    while any(going):
        for i, stream in enumerate(streams):
            if going[i]:
                going[i] = stream.advance()
    sent = [stream.sent for stream in streams]
    for work in waiting:
        sent = work(sent)
    for group in range(GROUPS - 1):
        sent = share_cores(group, sent)
        share_cores(group, sent, 0)
        sent = share_segments(group, sent)
        finish(group)
    for layer in reversed(range(1, layers)):
        for piece in last:
            sent = piece(layer, every)([sent, residuals.get(GROUPS - 2)] if layer == 1 and piece is last[-1] else sent)
    sent = share_cores(GROUPS - 1, sent)
    sent = share_segments(GROUPS - 1, sent)
    for piece in last:
        sent = piece(0, every)(sent)
    share_cores(GROUPS - 1, sent, 0)
    finish(GROUPS - 1)
    own = jnp.stack([residuals[group] for group in range(GROUPS)], axis=1)
    residual = targets[0].astype(F32) - own.reshape(targets.shape[1:])
    features = jnp.concatenate(
        [
            jnp.concatenate([finished[group, chunk] for chunk in range(CHUNKS)], axis=1)
            for group in range(GROUPS)
        ],
        axis=0,
    )
    return (features[None], residual[None])


def solution(mesh):
    in_specs = (
        P("segment", "feat", "tok"),
        P("segment", "tok", "feat"),
        P("segment", "feat", "tok"),
        P("segment", "tok"),
        P("segment", None, "feat", "tok"),
    )
    out_specs = (P("segment", "feat", "tok"), P("segment", "tok", "feat"))
    sizes = (mesh.shape["segment"], mesh.shape["feat"], mesh.shape["tok"])
    return jax.shard_map(
        lambda *args: local(*sizes, *args), mesh=mesh, in_specs=in_specs, out_specs=out_specs, check_vma=False
    )
```

```python
import jax
import jax.numpy as jnp
from jax import lax
from jax.sharding import PartitionSpec as P

BF16 = jnp.bfloat16
F32 = jnp.float32
GROUPS = 2
CHUNKS = 2
STREAMS = 2
PIECES = 2


def local(segments, ring, cores, layer_inputs, targets, enc_weight, enc_bias, dec_weight):
    z = lax.axis_index("feat")
    core = lax.axis_index("tok")
    segment = lax.axis_index("segment")
    odd = z % 2 == 1
    rows = layer_inputs.shape[1] // GROUPS
    width = enc_weight.shape[2] // CHUNKS
    depth = enc_weight.shape[1]
    weight = enc_weight[0]
    decoders = dec_weight[0]
    layers = decoders.shape[0]
    per_core = ring // cores


    swaps = ring & (ring - 1) == 0

    def exchanged():
        share = layer_inputs.shape[1] // cores
        halves = []
        for k in range(cores):
            half = lax.dynamic_slice_in_dim(layer_inputs[0], (core + k) % cores * share, share, axis=0)
            if k:
                half = lax.ppermute(half, "tok", [(i, (i + k) % cores) for i in range(cores)])
            halves.append(half)
        halves = jnp.stack(halves)
        block = jnp.concatenate(
            [lax.dynamic_index_in_dim(halves, (core - c) % cores, axis=0, keepdims=False) for c in range(cores)],
            axis=1,
        )
        parts = []
        for k in range(ring):
            to = z ^ k if swaps else (z + k) % ring
            part = lax.dynamic_slice_in_dim(block, to * depth, depth, axis=1)
            if k:
                pairs = [(i, i ^ k if swaps else (i + k) % ring) for i in range(ring)]
                part = lax.ppermute(part, "feat", pairs)
            parts.append(part)
        every = lax.all_gather(jnp.stack(parts), "tok", axis=1, tiled=True)
        order = [z ^ ((z - k) % ring) if swaps else k for k in range(ring)]
        every = [lax.dynamic_index_in_dim(every, i, axis=0, keepdims=False) for i in order]
        return [
            jnp.concatenate([part[group * rows : (group + 1) * rows] for part in every], axis=0)
            for group in range(GROUPS)
        ]

    columns = exchanged()

    def partial_sums(group, chunk, sent=None):
        part = jnp.dot(
            after(columns[group], sent), weight[:, chunk * width : (chunk + 1) * width], preferred_element_type=F32
        ).astype(BF16)
        return [part[k * rows : (k + 1) * rows] for k in range(ring)]

    units = [(group, chunk) for group in range(GROUPS) for chunk in range(CHUNKS)]
    finished = {}
    decoded = {}
    waiting = []
    ordered = [None]
    last = []
    totals = {}
    residuals = {}
    arrived = {}

    def after(values, others):
        others = [x for x in jax.tree.leaves(others) if x is not None]
        return lax.optimization_barrier((values, others))[0] if others else values

    def background(sent):
        ordered[0] = sent
        for _ in range(min(PIECES, len(waiting))):
            ordered[0] = sent = waiting.pop(0)(sent)

    every = list(range(ring))

    def decode(unit, own, got):
        group, chunk = unit
        codes = {}

        def selected(places, sent):
            used = {slot for m in places if m for slot in (m - 1, ring - m - 1)}
            needed = tuple({slot: came[slot] for slot in sorted(used & set(came))} for came in got)
            mine, (even, other) = after((own, needed), sent)
            zero = jnp.zeros_like(mine)
            parts = []
            for m in places:
                a, b = m - 1, ring - m - 1
                left = jnp.where(odd, even.get(a, zero), other.get(a, zero))
                right = jnp.where(odd, other.get(b, zero), even.get(b, zero))
                parts.append(jnp.where(m <= z, left, right) if m else mine)
            return jnp.concatenate(parts, axis=0)

        def piece(layer, places):
            def run(sent):
                key = tuple(places)
                if key not in codes:
                    codes[key] = selected(places, sent)
                out = lax.dot_general(
                    after(codes[key], sent),
                    decoders[layer, :, chunk * width : (chunk + 1) * width],
                    (((1,), (1,)), ((), ())),
                    preferred_element_type=F32,
                )
                key = group, layer
                decoded[key] = out if key not in decoded else decoded[key] + out
                return decoded[key]

            return run

        if group < GROUPS - 1:
            waiting.extend(piece(layer, every) for layer in reversed(range(layers)))
        else:
            last.append(piece)

    class Stream:
        def __init__(self, own):
            self.own = own
            self.step = 0
            self.slot = 1
            self.got = [{}, {}]
            self.sums = None

        def swap(self, value, side):
            i, k, n = self.step, self.slot, len(self.own)
            pairs = []
            for p in range(side, ring - 1, 2):
                q = ring - 2 - p
                if not (i == 0 and p >= k or i == n and p < k):
                    pairs.append((p, p + 1))
                if not (i == 0 and q >= k or i == n and q < k):
                    pairs.append((p + 1, p))
            return lax.ppermute(value, "feat", pairs) if pairs else None

        def advance(self):
            i, k, n = self.step, self.slot, len(self.own)
            if self.sums is None:
                self.sums = partial_sums(*self.own[0], ordered)
            sent = []
            for side in range(2):
                if k == 0:
                    sent.append(finished[self.own[i - 1]])
                    continue
                value = self.got[1 - side].get(k - 1)
                if value is not None:
                    value = after(value, ordered)
                if i < n:
                    rightward = odd == (side == 1)
                    zero = jnp.zeros_like(self.sums[k])
                    own = jnp.where(
                        rightward,
                        jnp.where(k > z, self.sums[k], zero),
                        jnp.where(k > ring - 1 - z, self.sums[ring - k], zero),
                    )
                    value = own if value is None else (own.astype(F32) + value.astype(F32)).astype(BF16)
                sent.append(value)
            for side in range(2):
                got = self.swap(sent[side], side) if sent[side] is not None else None
                if got is not None:
                    self.got[side][k] = got
            if i < n or k < ring - 2:
                background(sent)
            self.sent = sent
            if i and k == ring - 2:
                unit = self.own[i - 1]
                decode(unit, finished[unit], tuple(dict(got) for got in self.got))
            self.slot += 1
            if i < n and k == ring - 1:
                chunk = self.own[i][1]
                bias = enc_bias[0, chunk * width : (chunk + 1) * width][None, :]
                total = self.sums[0].astype(F32) + self.got[0][k].astype(F32) + self.got[1][k].astype(F32)
                finished[self.own[i]] = jax.nn.relu(total + bias).astype(BF16)
                self.slot, self.step = 0, i + 1
                if i + 1 < n:
                    self.sums = partial_sums(*self.own[i + 1])
                self.got = [{}, {}]
                return True
            return not (i == n and k == ring - 2)

    def share_cores(group, sent, first=1):
        blocks = after([decoded[group, layer] for layer in range(first, layers if first else 1)], sent)
        blocks = jnp.stack(blocks).reshape(-1, ring, rows, depth)

        def share(index):
            begin = index * per_core
            return jnp.stack(
                [
                    lax.dynamic_index_in_dim(blocks, (z - begin - b) % ring, axis=1, keepdims=False)
                    for b in range(per_core)
                ],
                axis=1,
            )

        total = share(core)
        given = []
        for k in range(1, cores):
            given.append(share((core + k) % cores).astype(BF16))
            got = lax.ppermute(given[-1], "tok", [(i, (i + k) % cores) for i in range(cores)])
            total += got.astype(F32)
        totals[group, first] = total
        return given

    def share_segments(group, sent):
        total = after(totals[group, 1], sent)
        paired = segments & (segments - 1) == 0
        received, given = [], []
        for k in range(1, segments):
            place = segment ^ k if paired else jnp.minimum(segment + k, layers - 1)
            given.append(lax.dynamic_index_in_dim(total, jnp.maximum(place, 1) - 1, axis=0, keepdims=False).astype(BF16))
            pairs = [(i, i ^ k if paired else i + k) for i in range(segments)]
            got = lax.ppermute(given[-1], "segment", [(i, j) for i, j in pairs if i < j < segments])
            received.append(got)
        arrived[group] = total, received
        return given

    def finish(group):
        total, received = arrived[group]
        own = jnp.where(
            segment == 0,
            totals[group, 0][0],
            lax.dynamic_index_in_dim(total, jnp.maximum(segment, 1) - 1, axis=0, keepdims=False),
        )
        residuals[group] = sum([got.astype(F32) for got in received], own)

    streams = [Stream(units[i::STREAMS]) for i in range(STREAMS)]
    going = [True] * STREAMS
    while any(going):
        for i, stream in enumerate(streams):
            if going[i]:
                going[i] = stream.advance()
    sent = [stream.sent for stream in streams]
    for work in waiting:
        sent = work(sent)
    for group in range(GROUPS - 1):
        sent = share_cores(group, sent)
        share_cores(group, sent, 0)
        sent = share_segments(group, sent)
        finish(group)
    for layer in reversed(range(1, layers)):
        for piece in last:
            sent = piece(layer, every)([sent, residuals.get(GROUPS - 2)] if layer == 1 and piece is last[-1] else sent)
    sent = share_cores(GROUPS - 1, sent)
    sent = share_segments(GROUPS - 1, sent)
    for piece in last:
        sent = piece(0, every)(sent)
    share_cores(GROUPS - 1, sent, 0)
    finish(GROUPS - 1)
    own = jnp.stack([residuals[group] for group in range(GROUPS)], axis=1)
    residual = targets[0].astype(F32) - own.reshape(targets.shape[1:])
    features = jnp.concatenate(
        [
            jnp.concatenate([finished[group, chunk] for chunk in range(CHUNKS)], axis=1)
            for group in range(GROUPS)
        ],
        axis=0,
    )
    return (features[None], residual[None])


def solution(mesh):
    in_specs = (
        P("segment", "feat", "tok"),
        P("segment", "tok", "feat"),
        P("segment", "feat", "tok"),
        P("segment", "tok"),
        P("segment", None, "feat", "tok"),
    )
    out_specs = (P("segment", "feat", "tok"), P("segment", "tok", "feat"))
    sizes = (mesh.shape["segment"], mesh.shape["feat"], mesh.shape["tok"])
    return jax.shard_map(
        lambda *args: local(*sizes, *args), mesh=mesh, in_specs=in_specs, out_specs=out_specs, check_vma=False
    )
```
